32 devices in a mesh: space: 8 (over z, y), tm: 4 (over x, core).
Axes of the slice: x: 2, y: 2, z: 4, core: 2. Of those that a mesh axis runs over, the one named last changes fastest.
Arguments:
- snapshots: bfloat16 [16384, 2048], P('space', 'tm'), as said below
- sketch: bfloat16 [2048, 256], P('tm'), may hold values from -0.125 to 0.125
- rotation: float32 [256, 256], replicated, may hold values from -0.375 to 0.375
Outputs:
- basis: float32 [16384, 256], P(('space', 'tm'))
- triangle: float32 [256, 256], replicated
The draws below stay inside these ranges and needn't reach their ends.
Inputs may be any that keep to these rules, and one draw needn't show every extreme that they name: `snapshots`: the sketch has full column rank.
All inputs are finite; a program needn't handle non-finite values.
Results may differ from the reference program's by a relative error of at most 0.0003.
Values sent between devices are 32-bit elements; how exact they have to be, the bound alone decides.
No kernel may reach another device: no remote copies, remote signals or barrier semaphores. Data moves between devices by JAX's collectives and lax.ppermute only.
A program may use at most 64 MiB of HBM per device.

```python
import math
import jax
import jax.numpy as jnp
from jax import lax

K = 256
NSNAP = 2048
NCELL = 16384


def draw_snapshots(key, part):
    keys = jax.random.split(key, 3)
    cells = jnp.arange(NCELL, dtype=jnp.float32)[:, None] / NCELL
    trend = 0.5 * jnp.exp(cells * math.log(3.0))
    rough = jnp.exp(jax.random.uniform(keys[1], (NCELL, 1), jnp.float32, math.log(0.5), math.log(2.0)))
    columns = jnp.exp(jax.random.uniform(keys[2], (1, NSNAP), jnp.float32, 0.0, math.log(10.0)))
    base = jax.random.normal(keys[0], (NCELL, NSNAP), jnp.float32)
    return (base * trend * rough * columns).astype(jnp.bfloat16)


def shard_levels(rng, dims, shards, low, top_value):
    gain = 1.0
    for position, blocks in shards:
        heights = jax.random.uniform(jax.random.fold_in(jax.random.fold_in(rng, 6), position), (blocks,), jnp.float32, low / len(shards), top_value / len(shards))
        gain = gain * jnp.repeat(jnp.exp(heights), dims[position] // blocks).reshape((-1,) + (1,) * (len(dims) - 1 - position))
    return gain


def normal_values(key, dims, width, most, cuts=(), kind=jnp.bfloat16):
    loudness = shard_levels(key, dims, cuts, -0.22, 0.18) if cuts else 1.0
    result = jax.random.normal(key, dims, jnp.float32) * width * loudness
    return jnp.minimum(jnp.maximum(result, -most), most).astype(kind)


def setup_inputs(seed: int = 0) -> dict:
    seeds = jax.random.split(jax.random.key(seed), 4)
    snapshots = draw_snapshots(jax.random.fold_in(seeds[3], 71), 0)
    sketch = normal_values(seeds[1], (NSNAP, K), NSNAP ** -0.5, 0.125, ((0, 4),))
    rotation = normal_values(seeds[2], (K, K), K ** -0.5, 0.375, (), jnp.float32)
    return {"snapshots": snapshots, "sketch": sketch, "rotation": rotation}


def reference(snapshots, sketch, rotation):
    sketched = jnp.dot(snapshots.astype(jnp.float32), sketch.astype(jnp.float32), preferred_element_type=jnp.float32)
    gram = lax.dot_general(sketched.astype(jnp.float32), sketched.astype(jnp.float32), (((0,), (0,)), ((), ())), precision=lax.Precision.HIGHEST, preferred_element_type=jnp.float32)
    lower = jnp.linalg.cholesky(gram)
    orthonormal = lax.linalg.triangular_solve(lower, sketched, left_side=False, lower=True, transpose_a=True)
    scale = jnp.sqrt(jnp.float32(NCELL))
    basis = scale * jnp.dot(orthonormal.astype(jnp.float32), rotation.astype(jnp.float32), precision=lax.Precision.HIGHEST, preferred_element_type=jnp.float32)
    triangle = lower.T / scale
    return (basis, triangle)
```

```python
import functools
import math

import jax
import jax.numpy as jnp
from jax import lax
from jax.experimental import pallas as pl
from jax.experimental.pallas import tpu as pltpu
from jax.sharding import PartitionSpec as P

F32, BF16 = jnp.float32, jnp.bfloat16
VMEM = pl.BlockSpec(memory_space=pltpu.VMEM)
SMEM = pl.BlockSpec(memory_space=pltpu.SMEM)
PANEL = 32


def params():
    return pltpu.CompilerParams(vmem_limit_bytes=40 << 20)


def partner(shard, axis, level):
    return lax.ppermute(shard, axis, [(i, i ^ 1 << level) for i in range(lax.axis_size(axis))])


def levels(axis):
    return lax.axis_size(axis).bit_length() - 1


def split(x):
    high = x.astype(BF16)
    rest = x - high.astype(F32)
    middle = rest.astype(BF16)
    low = (rest - middle.astype(F32)).astype(BF16)
    return high, middle, low


def product(x, y, dims):
    return lax.dot_general(x, y, (dims, ((), ())), preferred_element_type=F32)


def dot_parts(x, y, dims):
    x1, x2, x3 = split(x)
    y1, y2, y3 = split(y)
    small = product(x1, y3, dims) + product(x2, y2, dims) + product(x3, y1, dims)
    return product(x1, y1, dims) + (product(x1, y2, dims) + product(x2, y1, dims) + small)


def dot_stacked(x, y):
    x1, x2, x3 = split(x)
    y1, y2, y3 = split(y)
    left = jnp.concatenate([x1, x1, x2, x1, x2, x3], axis=0)
    right = jnp.concatenate([y1, y2, y1, y3, y2, y1], axis=0)
    return product(left, right, ((0,), (0,)))


def sketch_kernel(blocks_ref, snapshots_ref, sketch_ref, out_ref):
    out_ref[0] = jnp.dot(snapshots_ref[...], sketch_ref[...], preferred_element_type=F32)


def sketch_blocks(blocks, snapshots, sketch, rows):
    count, (depth, columns) = blocks.shape[0], sketch.shape
    return pl.pallas_call(
        sketch_kernel,
        grid_spec=pltpu.PrefetchScalarGridSpec(
            num_scalar_prefetch=1,
            grid=(count,),
            in_specs=[
                pl.BlockSpec((rows, depth), lambda i, blocks: (blocks[i], 0)),
                pl.BlockSpec((depth, columns), lambda i, blocks: (0, 0)),
            ],
            out_specs=pl.BlockSpec((1, rows, columns), lambda i, blocks: (i, 0, 0)),
        ),
        out_shape=jax.ShapeDtypeStruct((count, rows, columns), F32),
        compiler_params=params(),
        cost_estimate=pl.CostEstimate(
            flops=2 * count * rows * depth * columns,
            bytes_accessed=count * rows * (2 * depth + 4 * columns) + 2 * depth * columns,
            transcendentals=0,
        ),
    )(blocks, snapshots, sketch)


def gram_kernel(side_ref, kept_ref, arrived_ref, sketched_ref, keep_ref, send_ref):
    sketched = kept_ref[...] + arrived_ref[...]
    sketched_ref[...] = sketched
    high, middle, low = split(sketched)
    rows = ((0,), (0,))
    cross = product(high, middle, rows) + product(high, low, rows)
    gram = product(high, high, rows) + (cross + cross.T + product(middle, middle, rows))
    h = gram.shape[0] // 2
    row = lax.broadcasted_iota(jnp.int32, (h, h), 0)
    column = lax.broadcasted_iota(jnp.int32, (h, h), 1)
    corner = gram[h:, h:]
    diagonal = jnp.sum(jnp.where(row == column, corner, 0.0), axis=0, keepdims=True)
    mixed = jnp.where(row >= column, gram[:h, :h], corner)
    first = side_ref[0] == 0
    keep_ref[:h, :] = jnp.where(first, gram[h:, :h], mixed)
    send_ref[:h, :] = jnp.where(first, mixed, gram[h:, :h])
    keep_ref[h:, :] = jnp.broadcast_to(diagonal, (8, h))
    send_ref[h:, :] = jnp.broadcast_to(diagonal, (8, h))


def gram_halves(side, kept, arrived):
    rows, n = kept.shape
    half = jax.ShapeDtypeStruct((n // 2 + 8, n // 2), F32)
    return pl.pallas_call(
        gram_kernel,
        out_shape=[jax.ShapeDtypeStruct((rows, n), F32), half, half],
        in_specs=[SMEM, VMEM, VMEM],
        out_specs=[VMEM] * 3,
        compiler_params=params(),
        cost_estimate=pl.CostEstimate(
            flops=8 * rows * n * n, bytes_accessed=12 * rows * n + 4 * n * n, transcendentals=0
        ),
    )(side, kept, arrived)


def inverse_root(x):
    y = lax.rsqrt(x)
    return y * (1.5 - 0.5 * x * y * y)


def factor(a, upper, inverse):
    n = a.shape[0]
    lane = lax.broadcasted_iota(jnp.int32, (8, n), 1)
    sub = lax.broadcasted_iota(jnp.int32, (8, n), 0)
    lane1 = lax.broadcasted_iota(jnp.int32, (8, 128), 1)
    sub1 = lax.broadcasted_iota(jnp.int32, (8, 128), 0)
    groups = PANEL // 8

    def wide(v):
        return jnp.concatenate([v] * (n // 128), axis=1)

    def column(v, c):
        return jnp.broadcast_to(v[:, c : c + 1], (8, 128))

    def row(v, k):
        return jnp.broadcast_to(v[k : k + 1, :], (8, v.shape[1]))

    for start in range(0, n, PANEL):
        tile = start // 128
        t = [a[start + 8 * i : start + 8 * i + 8, :] for i in range(groups)]
        e = [jnp.where(lane1 + 128 * tile == sub1 + (start + 8 * i), 1.0, 0.0) for i in range(groups)]
        for q in range(groups):
            c0 = start + 8 * q
            c = [column(t[q], c0 + j) for j in range(8)]
            s = {(k, j): row(c[j], k) for j in range(8) for k in range(j, 8)}
            r, m = {}, {}
            for j in range(8):
                r[j] = inverse_root(s[j, j])
                for k in range(j + 1, 8):
                    m[k, j] = s[k, j] * r[j]
                for k in range(j + 1, 8):
                    for i in range(j + 1, k + 1):
                        s[k, i] = s[k, i] - m[k, j] * m[i, j]
            pt = [row(t[q], j) for j in range(8)]
            pe = [row(e[q], j) for j in range(8)]
            for j in range(8):
                pt[j] = pt[j] * wide(r[j])
                pe[j] = pe[j] * r[j]
                for k in range(j + 1, 8):
                    pt[k] = pt[k] - wide(m[k, j]) * pt[j]
                    pe[k] = pe[k] - m[k, j] * pe[j]
            for i in range(q + 1, groups):
                c = [column(t[i], c0 + j) for j in range(8)]
                for j in range(8):
                    c[j] = c[j] * r[j]
                    for k in range(j + 1, 8):
                        c[k] = c[k] - c[j] * m[k, j]
                for j in range(8):
                    t[i] = t[i] - wide(c[j]) * pt[j]
                    e[i] = e[i] - c[j] * pe[j]
            tq, eq = pt[0], pe[0]
            for j in range(1, 8):
                tq = jnp.where(sub == j, pt[j], tq)
                eq = jnp.where(sub1 == j, pe[j], eq)
            t[q], e[q] = tq, eq
        done = (lane >= start) & (lane < start + PANEL)
        mixed = []
        for i in range(groups):
            top = start + 8 * i
            parts = [jnp.zeros((8, 128), F32)] * (n // 128)
            parts[tile] = e[i]
            own = jnp.concatenate(parts, axis=1)
            upper[top : top + 8, :] = jnp.where(lane >= sub + top, t[i], 0.0)
            inverse[top : top + 8, :] = jnp.where(lane < start, t[i], own)
            mixed.append(jnp.where(done, own, t[i]))
        after = start + PANEL
        if after < n:
            base = after // 128 * 128
            left = jnp.concatenate([v[:, base:] for v in t], axis=0)
            update = dot_stacked(left, jnp.concatenate(mixed, axis=0))
            for top in range(after, n, 8):
                old = jnp.where(done, 0.0, a[top : top + 8, :])
                a[top : top + 8, :] = old - update[top - base : top - base + 8, :]


def basis_kernel(scale, side_ref, mine_ref, other_ref, rotation_ref, sketched_ref, basis_ref, triangle_ref, a, upper, inverse):
    n = a.shape[0]
    h = n // 2
    first = side_ref[0] == 0
    mine, other = mine_ref[...], other_ref[...]
    below = jnp.where(first, mine[:h, :], other[:h, :])
    mixed = jnp.where(first, other[:h, :], mine[:h, :])
    flipped = mixed.T
    row = lax.broadcasted_iota(jnp.int32, (h, h), 0)
    column = lax.broadcasted_iota(jnp.int32, (h, h), 1)
    diagonal = jnp.broadcast_to(mine[h : h + 1, :], (h, h))
    a[:h, :h] = jnp.where(row >= column, mixed, flipped)
    a[h:, :h] = below
    a[:h, h:] = below.T
    a[h:, h:] = jnp.where(row < column, mixed, jnp.where(row > column, flipped, diagonal))
    factor(a, upper, inverse)
    triangle_ref[...] = upper[...] * (1.0 / scale)
    mapping = dot_parts(inverse[...], scale * rotation_ref[...], ((0,), (0,)))
    basis_ref[...] = dot_parts(sketched_ref[...], mapping, ((1,), (0,)))


def basis_and_triangle(side, mine, other, rotation, sketched, scale):
    (rows, n) = sketched.shape
    return pl.pallas_call(
        functools.partial(basis_kernel, scale),
        out_shape=[jax.ShapeDtypeStruct((rows, n), F32), jax.ShapeDtypeStruct((n, n), F32)],
        in_specs=[SMEM, VMEM, VMEM, VMEM, VMEM],
        out_specs=[VMEM] * 2,
        scratch_shapes=[pltpu.VMEM((n, n), F32)] * 3,
        compiler_params=params(),
        cost_estimate=pl.CostEstimate(
            flops=12 * rows * n * n + 40 * n * n * n, bytes_accessed=8 * rows * n + 12 * n * n, transcendentals=n
        ),
    )(side, mine, other, rotation, sketched)


def shards(snapshots, sketch, rotation):
    groups, depth = lax.axis_size("tm"), levels("tm")
    rows = snapshots.shape[0] // groups
    cells = snapshots.shape[0] * lax.axis_size("space")
    index = lax.axis_index("tm").astype(jnp.int32)
    side = (index & 1).reshape(1)

    def masks(low):
        half = groups // 2
        return jnp.array(
            [low | sum((1 - (p >> (depth - 1 - l) & 1)) << l for l in range(1, depth)) for p in range(half)], jnp.int32
        )

    leaving = sketch_blocks(index ^ masks(1), snapshots, sketch, rows)
    arrived = partner(leaving, "tm", 0)
    kept = sketch_blocks(index ^ masks(0), snapshots, sketch, rows)
    for level in range(1, depth):
        middle = kept.shape[0] // 2
        leaving = kept[:middle] + arrived[:middle]
        kept = kept[middle:] + arrived[middle:]
        arrived = partner(leaving, "tm", level)
    sketched, mine, send = gram_halves(side, kept[0], arrived[0])
    mine = mine + partner(send, "tm", 0)
    for level in range(1, depth):
        mine = mine + partner(mine, "tm", level)
    for level in range(levels("space")):
        mine = mine + partner(mine, "space", level)
    other = partner(mine, "tm", 0)
    return tuple(basis_and_triangle(side, mine, other, rotation, sketched, math.sqrt(cells)))


def solution(mesh):
    in_specs = (P("space", "tm"), P("tm", None), P())
    out_specs = (P(("space", "tm"), None), P())
    return jax.shard_map(shards, mesh=mesh, in_specs=in_specs, out_specs=out_specs, check_vma=False)
```

```python
import functools
import math

import jax
import jax.numpy as jnp
from jax import lax
from jax.experimental import pallas as pl
from jax.experimental.pallas import tpu as pltpu
from jax.sharding import PartitionSpec as P

F32, BF16 = jnp.float32, jnp.bfloat16
VMEM = pl.BlockSpec(memory_space=pltpu.VMEM)
SMEM = pl.BlockSpec(memory_space=pltpu.SMEM)
BLOCK = 64
PANEL = 2


def params():
    return pltpu.CompilerParams(vmem_limit_bytes=40 << 20)


def partner(shard, axis, level):
    return lax.ppermute(shard, axis, [(i, i ^ 1 << level) for i in range(lax.axis_size(axis))])


def levels(axis):
    return lax.axis_size(axis).bit_length() - 1


def split(x):
    high = x.astype(BF16)
    rest = x - high.astype(F32)
    middle = rest.astype(BF16)
    low = (rest - middle.astype(F32)).astype(BF16)
    return high, middle, low


def product(x, y, dims):
    return lax.dot_general(x, y, (dims, ((), ())), preferred_element_type=F32)


def dot_parts(x, y, dims):
    x1, x2, x3 = split(x)
    y1, y2, y3 = split(y)
    small = product(x1, y3, dims) + product(x2, y2, dims) + product(x3, y1, dims)
    return product(x1, y1, dims) + (product(x1, y2, dims) + product(x2, y1, dims) + small)


PIECES = 4


def sketch_kernel(masks, snapshots_ref, sketch_ref, *rest):
    outs, (tall, wide, arrived, ready) = rest[: len(masks)], rest[len(masks) :]
    rows, step = tall.shape[0] // len(masks), tall.shape[0] // len(masks) // PIECES
    index = lax.axis_index("tm")
    fetch = pltpu.make_async_copy(sketch_ref, wide, ready)
    fetch.start()
    copies = []
    for i, mask in enumerate(masks):
        start = pl.multiple_of((index ^ mask) * rows, rows)
        for j in range(PIECES):
            copies.append(
                pltpu.make_async_copy(
                    snapshots_ref.at[pl.ds(start + step * j, step)],
                    tall.at[pl.ds(rows * i + step * j, step)],
                    arrived.at[PIECES * i + j],
                )
            )
            copies[-1].start()
    fetch.wait()
    for i, out in enumerate(outs):
        for j in range(PIECES):
            copies[PIECES * i + j].wait()
            block = tall[rows * i + step * j : rows * i + step * (j + 1), :]
            out[step * j : step * (j + 1), :] = jnp.dot(block, wide[...], preferred_element_type=F32)


def sketch_blocks(masks, snapshots, sketch):
    rows = snapshots.shape[0] // lax.axis_size("tm")
    depth, columns = sketch.shape
    count = len(masks)
    return pl.pallas_call(
        functools.partial(sketch_kernel, masks),
        out_shape=[jax.ShapeDtypeStruct((rows, columns), F32)] * count,
        in_specs=[pl.BlockSpec(memory_space=pltpu.HBM)] * 2,
        out_specs=[VMEM] * count,
        scratch_shapes=[
            pltpu.VMEM((count * rows, depth), BF16),
            pltpu.VMEM((depth, columns), BF16),
            pltpu.SemaphoreType.DMA((PIECES * count,)),
            pltpu.SemaphoreType.DMA,
        ],
        compiler_params=params(),
        cost_estimate=pl.CostEstimate(
            flops=2 * count * rows * depth * columns,
            bytes_accessed=count * rows * (2 * depth + 4 * columns) + 2 * depth * columns,
            transcendentals=0,
        ),
    )(snapshots, sketch)


def gram_kernel(side_ref, kept_ref, near_ref, far_ref, sketched_ref, keep_ref, send_ref):
    sketched = (kept_ref[...] + near_ref[...]) + far_ref[...]
    sketched_ref[...] = sketched
    high, middle, low = split(sketched)
    rows = ((0,), (0,))
    cross = product(high, middle, rows) + product(high, low, rows)
    gram = product(high, high, rows) + (cross + cross.T + product(middle, middle, rows))
    h = gram.shape[0] // 2
    row = lax.broadcasted_iota(jnp.int32, (h, h), 0)
    column = lax.broadcasted_iota(jnp.int32, (h, h), 1)
    corner = gram[h:, h:]
    diagonal = jnp.sum(jnp.where(row == column, corner, 0.0), axis=0, keepdims=True)
    mixed = jnp.where(row >= column, gram[:h, :h], corner)
    first = side_ref[0] == 0
    keep_ref[:h, :] = jnp.where(first, gram[h:, :h], mixed)
    send_ref[:h, :] = jnp.where(first, mixed, gram[h:, :h])
    keep_ref[h:, :] = jnp.broadcast_to(diagonal, (8, h))
    send_ref[h:, :] = jnp.broadcast_to(diagonal, (8, h))


def gram_halves(side, kept, near, far):
    rows, n = kept.shape
    half = jax.ShapeDtypeStruct((n // 2 + 8, n // 2), F32)
    return pl.pallas_call(
        gram_kernel,
        out_shape=[jax.ShapeDtypeStruct((rows, n), F32), half, half],
        in_specs=[SMEM, VMEM, VMEM, VMEM],
        out_specs=[VMEM] * 3,
        compiler_params=params(),
        cost_estimate=pl.CostEstimate(
            flops=8 * rows * n * n, bytes_accessed=16 * rows * n + 4 * n * n, transcendentals=0
        ),
    )(side, kept, near, far)


def column(v, c):
    return jnp.broadcast_to(v[:, c : c + 1], (8, 128))


def row(v, k):
    return jnp.broadcast_to(v[k : k + 1, :], (8, 128))


def stacked(x, order):
    parts = split(x)
    return jnp.concatenate([parts[i] for i in order], axis=0)


def factor(a, upper, inverse):
    n = a.shape[0]
    tiles = n // 128
    lane = lax.broadcasted_iota(jnp.int32, (8, 128), 1)
    sub = lax.broadcasted_iota(jnp.int32, (8, 128), 0)
    groups, width = BLOCK // 8, 8 * PANEL
    zero = jnp.zeros((8, 128), F32)
    for start in range(0, n, BLOCK):
        tile, offset = divmod(start, 128)
        t = []
        for i in range(groups):
            top = start + 8 * i
            t.append([a[top : top + 8, 128 * x : 128 * x + 128] for x in range(tiles)])
            t[i].append(jnp.where(lane == sub + (offset + 8 * i), 1.0, 0.0))
        for q in range(0, groups, PANEL):
            first = offset + 8 * q
            c = {(g, j): column(t[q + g][tile], first + j) for g in range(PANEL) for j in range(8 * g + 8)}
            r, l, m = {}, {}, {}
            pivot = row(c[0, 0], 0)
            for j in range(width):
                r[j] = lax.rsqrt(pivot)
                if j + 1 < width:
                    g, k = divmod(j + 1, 8)
                    m[j + 1, j] = row(c[g, j], k) * r[j]
                    pivot = row(c[g, j + 1], k) - m[j + 1, j] * m[j + 1, j]
                for g in range(j // 8, PANEL):
                    l[g, j] = c[g, j] * r[j]
                for k in range(j + 1, width):
                    if k > j + 1:
                        m[k, j] = row(l[k // 8, j], k % 8)
                    for g in range(k // 8, PANEL):
                        c[g, k] = c[g, k] - l[g, j] * m[k, j]
            p = {}
            for g in range(PANEL):
                mine = t[q + g]
                for j in range(8 * g):
                    mine = [x - l[g, j] * y for x, y in zip(mine, p[j])]
                roots = r[8 * g]
                for jj in range(8):
                    j = 8 * g + jj
                    p[j] = [row(x, jj) * r[j] for x in mine]
                    below = jnp.where(sub > jj, l[g, j], 0.0)
                    mine = [x - below * y for x, y in zip(mine, p[j])]
                    roots = jnp.where(sub == jj, r[j], roots)
                t[q + g] = [x * roots for x in mine]
            for i in range(q + PANEL, groups):
                for g in range(PANEL):
                    c = [column(t[i][tile], first + 8 * g + jj) for jj in range(8)]
                    for jj in range(8):
                        c[jj] = c[jj] * r[8 * g + jj]
                        for kk in range(jj + 1, 8):
                            c[kk] = c[kk] - c[jj] * m[8 * g + kk, 8 * g + jj]
                    for jj in range(8):
                        t[i] = [x - c[jj] * y for x, y in zip(t[i], p[8 * g + jj])]
        done = (lane >= offset) & (lane < offset + BLOCK)
        left, right = [[] for _ in range(tiles)], [[] for _ in range(tiles)]
        for i in range(groups):
            top, own = start + 8 * i, t[i][tiles]
            for x in range(tiles):
                u = w = z = t[i][x]
                if x < tile:
                    u = zero
                elif x > tile:
                    w = zero
                else:
                    u = jnp.where(lane >= sub + (offset + 8 * i), u, 0.0)
                    w = jnp.where(lane < offset, w, own)
                    z = jnp.where(done, own, z)
                upper[top : top + 8, 128 * x : 128 * x + 128] = u
                inverse[top : top + 8, 128 * x : 128 * x + 128] = w
                left[x].append(u)
                right[x].append(z)
        after = start + BLOCK
        if after < n:
            y = stacked(jnp.concatenate([jnp.concatenate(v, axis=0) for v in right], axis=1), (0, 1, 0, 2, 1, 0))
            for x in range(after // 128, tiles):
                update = product(stacked(jnp.concatenate(left[x], axis=0), (0, 0, 1, 0, 1, 2)), y, ((0,), (0,)))
                for top in range(max(after, 128 * x), 128 * x + 128, 8):
                    for k in range(tiles):
                        old = a[top : top + 8, 128 * k : 128 * k + 128]
                        if k == tile:
                            old = jnp.where(done, 0.0, old)
                        new = update[top - 128 * x : top - 128 * x + 8, 128 * k : 128 * k + 128]
                        a[top : top + 8, 128 * k : 128 * k + 128] = old - new


def basis_kernel(scale, side_ref, mine_ref, other_ref, rotation_ref, sketched_ref, basis_ref, triangle_ref, a, upper, inverse):
    n = a.shape[0]
    h = n // 2
    first = side_ref[0] == 0
    mine, other = mine_ref[...], other_ref[...]
    below = jnp.where(first, mine[:h, :], other[:h, :])
    mixed = jnp.where(first, other[:h, :], mine[:h, :])
    flipped = mixed.T
    row = lax.broadcasted_iota(jnp.int32, (h, h), 0)
    column = lax.broadcasted_iota(jnp.int32, (h, h), 1)
    diagonal = jnp.broadcast_to(mine[h : h + 1, :], (h, h))
    a[:h, :h] = jnp.where(row >= column, mixed, flipped)
    a[h:, :h] = below
    a[:h, h:] = below.T
    a[h:, h:] = jnp.where(row < column, mixed, jnp.where(row > column, flipped, diagonal))
    factor(a, upper, inverse)
    triangle_ref[...] = upper[...] * (1.0 / scale)
    mapping = dot_parts(inverse[...], scale * rotation_ref[...], ((0,), (0,)))
    basis_ref[...] = dot_parts(sketched_ref[...], mapping, ((1,), (0,)))


def basis_and_triangle(side, mine, other, rotation, sketched, scale):
    (rows, n) = sketched.shape
    return pl.pallas_call(
        functools.partial(basis_kernel, scale),
        out_shape=[jax.ShapeDtypeStruct((rows, n), F32), jax.ShapeDtypeStruct((n, n), F32)],
        in_specs=[SMEM, VMEM, VMEM, VMEM, VMEM],
        out_specs=[VMEM] * 2,
        scratch_shapes=[pltpu.VMEM((n, n), F32)] * 3,
        compiler_params=params(),
        cost_estimate=pl.CostEstimate(
            flops=12 * rows * n * n + 40 * n * n * n, bytes_accessed=8 * rows * n + 12 * n * n, transcendentals=n
        ),
    )(side, mine, other, rotation, sketched)


def shards(snapshots, sketch, rotation):
    depth = levels("tm")
    cells = snapshots.shape[0] * lax.axis_size("space")
    side = (lax.axis_index("tm").astype(jnp.int32) & 1).reshape(1)

    kept, near = {}, {}
    for mask in range(lax.axis_size("tm") - 2, -1, -2):
        if mask:
            (leaving,) = sketch_blocks([mask | 1], snapshots, sketch)
            (kept[mask],) = sketch_blocks([mask], snapshots, sketch)
        else:
            leaving, kept[mask] = sketch_blocks([mask | 1, mask], snapshots, sketch)
        near[mask] = partner(leaving, "tm", 0)
    for level in range(1, depth):
        for mask in [m for m in kept if m >> level & 1]:
            arrived = partner(kept.pop(mask) + near.pop(mask), "tm", level)
            stays = mask ^ 1 << level
            near[stays] = near[stays] + arrived if level < depth - 1 else near[stays]
    sketched, mine, send = gram_halves(side, kept[0], near[0], arrived)
    mine = mine + partner(send, "tm", 0)
    for level in range(1, depth):
        mine = mine + partner(mine, "tm", level)
    for level in range(levels("space")):
        mine = mine + partner(mine, "space", level)
    other = partner(mine, "tm", 0)
    return tuple(basis_and_triangle(side, mine, other, rotation, sketched, math.sqrt(cells)))


def solution(mesh):
    in_specs = (P("space", "tm"), P("tm", None), P())
    out_specs = (P(("space", "tm"), None), P())
    return jax.shard_map(shards, mesh=mesh, in_specs=in_specs, out_specs=out_specs, check_vma=False)
```

```python
import functools
import math

import jax
import jax.numpy as jnp
from jax import lax
from jax.experimental import pallas as pl
from jax.experimental.pallas import tpu as pltpu
from jax.sharding import PartitionSpec as P

F32, BF16 = jnp.float32, jnp.bfloat16
VMEM = pl.BlockSpec(memory_space=pltpu.VMEM)
SMEM = pl.BlockSpec(memory_space=pltpu.SMEM)
BLOCK = 64
PANEL = 2


def params(mib=40):
    return pltpu.CompilerParams(vmem_limit_bytes=int(mib * 2**20))


def partner(shard, axis, level):
    return lax.ppermute(shard, axis, [(i, i ^ 1 << level) for i in range(lax.axis_size(axis))])


def levels(axis):
    return lax.axis_size(axis).bit_length() - 1


def split(x):
    high = x.astype(BF16)
    rest = x - high.astype(F32)
    middle = rest.astype(BF16)
    low = (rest - middle.astype(F32)).astype(BF16)
    return high, middle, low


def product(x, y, dims):
    return lax.dot_general(x, y, (dims, ((), ())), preferred_element_type=F32)


def dot_parts(x, y, dims):
    x1, x2, x3 = split(x)
    y1, y2, y3 = split(y)
    small = product(x1, y3, dims) + product(x2, y2, dims) + product(x3, y1, dims)
    return product(x1, y1, dims) + (product(x1, y2, dims) + product(x2, y1, dims) + small)


PIECES = 1


def sketch_kernel(masks, keep, snapshots_ref, sketch_ref, *rest):
    *outs, tall, wide, arrived, ready = rest
    held = outs.pop() if keep else None
    rows, step = tall.shape[0] // len(masks), tall.shape[0] // len(masks) // PIECES
    index = lax.axis_index("tm")
    fetch = pltpu.make_async_copy(sketch_ref, wide, ready)
    fetch.start()
    copies = []
    for i, mask in enumerate(masks):
        start = pl.multiple_of((index ^ mask) * rows, rows)
        for j in range(PIECES):
            copies.append(
                pltpu.make_async_copy(
                    snapshots_ref.at[pl.ds(start + step * j, step)],
                    tall.at[pl.ds(rows * i + step * j, step)],
                    arrived.at[PIECES * i + j],
                )
            )
            copies[-1].start()
    fetch.wait()
    if keep:
        held[...] = wide[...]
    for i, out in enumerate(outs):
        for j in range(PIECES):
            copies[PIECES * i + j].wait()
            block = tall[rows * i + step * j : rows * i + step * (j + 1), :]
            out[step * j : step * (j + 1), :] = jnp.dot(block, wide[...], preferred_element_type=F32)


def sketch_blocks(masks, snapshots, sketch, keep=False):
    rows = snapshots.shape[0] // lax.axis_size("tm")
    depth, columns = sketch.shape
    count = len(masks)
    return pl.pallas_call(
        functools.partial(sketch_kernel, masks, keep),
        out_shape=[jax.ShapeDtypeStruct((rows, columns), F32)] * count
        + [jax.ShapeDtypeStruct((depth, columns), BF16)] * keep,
        in_specs=[pl.BlockSpec(memory_space=pltpu.HBM)] * 2,
        out_specs=[VMEM] * (count + keep),
        scratch_shapes=[
            pltpu.VMEM((count * rows, depth), BF16),
            pltpu.VMEM((depth, columns), BF16),
            pltpu.SemaphoreType.DMA((PIECES * count,)),
            pltpu.SemaphoreType.DMA,
        ],
        compiler_params=params(53.5 if keep else 52),
        cost_estimate=pl.CostEstimate(
            flops=2 * count * rows * depth * columns,
            bytes_accessed=count * rows * (2 * depth + 4 * columns) + 2 * depth * columns,
            transcendentals=0,
        ),
    )(snapshots, sketch)


def gram_kernel(side_ref, kept_ref, near_ref, far_ref, sketched_ref, keep_ref, send_ref):
    sketched = (kept_ref[...] + near_ref[...]) + far_ref[...]
    sketched_ref[...] = sketched
    high, middle, low = split(sketched)
    rows = ((0,), (0,))
    cross = product(high, middle, rows) + product(high, low, rows)
    gram = product(high, high, rows) + (cross + cross.T + product(middle, middle, rows))
    h = gram.shape[0] // 2
    row = lax.broadcasted_iota(jnp.int32, (h, h), 0)
    column = lax.broadcasted_iota(jnp.int32, (h, h), 1)
    corner = gram[h:, h:]
    diagonal = jnp.sum(jnp.where(row == column, corner, 0.0), axis=0, keepdims=True)
    mixed = jnp.where(row >= column, gram[:h, :h], corner)
    first = side_ref[0] == 0
    keep_ref[:h, :] = jnp.where(first, gram[h:, :h], mixed)
    send_ref[:h, :] = jnp.where(first, mixed, gram[h:, :h])
    keep_ref[h:, :] = jnp.broadcast_to(diagonal, (8, h))
    send_ref[h:, :] = jnp.broadcast_to(diagonal, (8, h))


def gram_halves(side, kept, near, far):
    rows, n = kept.shape
    half = jax.ShapeDtypeStruct((n // 2 + 8, n // 2), F32)
    return pl.pallas_call(
        gram_kernel,
        out_shape=[jax.ShapeDtypeStruct((rows, n), F32), half, half],
        in_specs=[SMEM, VMEM, VMEM, VMEM],
        out_specs=[VMEM] * 3,
        compiler_params=params(),
        cost_estimate=pl.CostEstimate(
            flops=8 * rows * n * n, bytes_accessed=16 * rows * n + 4 * n * n, transcendentals=0
        ),
    )(side, kept, near, far)


def column(v, c):
    return jnp.broadcast_to(v[:, c : c + 1], (8, 128))


def row(v, k):
    return jnp.broadcast_to(v[k : k + 1, :], (8, 128))


def stacked(x, order):
    parts = split(x)
    return jnp.concatenate([parts[i] for i in order], axis=0)


def factor(a, upper, inverse):
    n = a.shape[0]
    tiles = n // 128
    lane = lax.broadcasted_iota(jnp.int32, (8, 128), 1)
    sub = lax.broadcasted_iota(jnp.int32, (8, 128), 0)
    groups, width = BLOCK // 8, 8 * PANEL
    zero = jnp.zeros((8, 128), F32)
    for start in range(0, n, BLOCK):
        tile, offset = divmod(start, 128)
        t = []
        for i in range(groups):
            top = start + 8 * i
            t.append([a[top : top + 8, 128 * x : 128 * x + 128] for x in range(tiles)])
            t[i].append(jnp.where(lane == sub + (offset + 8 * i), 1.0, 0.0))
        for q in range(0, groups, PANEL):
            first = offset + 8 * q
            c = {(g, j): column(t[q + g][tile], first + j) for g in range(PANEL) for j in range(8 * g + 8)}
            r, l, m = {}, {}, {}
            pivot = row(c[0, 0], 0)
            for j in range(width):
                r[j] = lax.rsqrt(pivot)
                if j + 1 < width:
                    g, k = divmod(j + 1, 8)
                    m[j + 1, j] = row(c[g, j], k) * r[j]
                    pivot = row(c[g, j + 1], k) - m[j + 1, j] * m[j + 1, j]
                for g in range(j // 8, PANEL):
                    l[g, j] = c[g, j] * r[j]
                for k in range(j + 1, width):
                    if k > j + 1:
                        m[k, j] = row(l[k // 8, j], k % 8)
                    for g in range(k // 8, PANEL):
                        c[g, k] = c[g, k] - l[g, j] * m[k, j]
            p = {}
            for g in range(PANEL):
                mine = t[q + g]
                for j in range(8 * g):
                    mine = [x - l[g, j] * y for x, y in zip(mine, p[j])]
                roots = r[8 * g]
                for jj in range(8):
                    j = 8 * g + jj
                    p[j] = [row(x, jj) * r[j] for x in mine]
                    below = jnp.where(sub > jj, l[g, j], 0.0)
                    mine = [x - below * y for x, y in zip(mine, p[j])]
                    roots = jnp.where(sub == jj, r[j], roots)
                t[q + g] = [x * roots for x in mine]
            for i in range(q + PANEL, groups):
                for g in range(PANEL):
                    c = [column(t[i][tile], first + 8 * g + jj) for jj in range(8)]
                    for jj in range(8):
                        c[jj] = c[jj] * r[8 * g + jj]
                        for kk in range(jj + 1, 8):
                            c[kk] = c[kk] - c[jj] * m[8 * g + kk, 8 * g + jj]
                    for jj in range(8):
                        t[i] = [x - c[jj] * y for x, y in zip(t[i], p[8 * g + jj])]
        done = (lane >= offset) & (lane < offset + BLOCK)
        left, right = [[] for _ in range(tiles)], [[] for _ in range(tiles)]
        for i in range(groups):
            top, own = start + 8 * i, t[i][tiles]
            for x in range(tiles):
                u = w = z = t[i][x]
                if x < tile:
                    u = zero
                elif x > tile:
                    w = zero
                else:
                    u = jnp.where(lane >= sub + (offset + 8 * i), u, 0.0)
                    w = jnp.where(lane < offset, w, own)
                    z = jnp.where(done, own, z)
                upper[top : top + 8, 128 * x : 128 * x + 128] = u
                inverse[top : top + 8, 128 * x : 128 * x + 128] = w
                left[x].append(u)
                right[x].append(z)
        after = start + BLOCK
        if after < n:
            y = stacked(jnp.concatenate([jnp.concatenate(v, axis=0) for v in right], axis=1), (0, 1, 0, 2, 1, 0))
            for x in range(after // 128, tiles):
                update = product(stacked(jnp.concatenate(left[x], axis=0), (0, 0, 1, 0, 1, 2)), y, ((0,), (0,)))
                for top in range(max(after, 128 * x), 128 * x + 128, 8):
                    for k in range(tiles):
                        old = a[top : top + 8, 128 * k : 128 * k + 128]
                        if k == tile:
                            old = jnp.where(done, 0.0, old)
                        new = update[top - 128 * x : top - 128 * x + 8, 128 * k : 128 * k + 128]
                        a[top : top + 8, 128 * k : 128 * k + 128] = old - new


def triangles(shape):
    row = lax.broadcasted_iota(jnp.int32, shape, 0)
    column = lax.broadcasted_iota(jnp.int32, shape, 1)
    return row > column, row == column


def first_kernel(side_ref, mine_ref, out_ref, a, upper, inverse):
    h = a.shape[0]
    lower, middle = triangles((h, h))

    @pl.when(side_ref[0] == 1)
    def _():
        mixed = mine_ref[:h, :]
        a[...] = jnp.where(lower | middle, mixed, mixed.T)
        factor(a, upper, inverse)
        out_ref[:h, :] = jnp.where(lower | middle, inverse[...], upper[...])
        diagonal = jnp.sum(jnp.where(middle, upper[...], 0.0), axis=0, keepdims=True)
        out_ref[h:, :] = jnp.broadcast_to(diagonal, (8, h))

    @pl.when(side_ref[0] == 0)
    def _():
        out_ref[...] = jnp.zeros_like(out_ref)


def first_factor(side, mine):
    h = mine.shape[1]
    return pl.pallas_call(
        first_kernel,
        out_shape=jax.ShapeDtypeStruct(mine.shape, F32),
        in_specs=[SMEM, VMEM],
        out_specs=VMEM,
        scratch_shapes=[pltpu.VMEM((h, h), F32)] * 3,
        compiler_params=params(),
        cost_estimate=pl.CostEstimate(flops=10 * h * h * h, bytes_accessed=8 * h * h, transcendentals=h),
    )(side, mine)


def basis_kernel(
    scale, side_ref, mine_ref, other_ref, own_ref, sent_ref, rotation_ref, sketched_ref, basis_ref, triangle_ref, a, upper, inverse
):
    h = a.shape[0]
    lower, middle = triangles((h, h))
    first = side_ref[0] == 0
    mine, other = mine_ref[...], other_ref[...]
    below = jnp.where(first, mine[:h, :], other[:h, :])
    mixed = jnp.where(first, other[:h, :], mine[:h, :])
    factors = jnp.where(first, sent_ref[...], own_ref[...])
    inverse1 = jnp.where(lower | middle, factors[:h, :], 0.0)
    upper1 = jnp.where(lower, 0.0, jnp.where(middle, factors[h : h + 1, :], factors[:h, :]))
    corner = jnp.where(lower, mixed.T, jnp.where(middle, mine[h : h + 1, :], mixed))
    left = dot_parts(below, inverse1, ((1,), (1,)))
    a[...] = corner - dot_parts(left, left, ((1,), (1,)))
    ahead = dot_parts(left, inverse1, ((1,), (0,)))
    x1, x2 = sketched_ref[:, :h], sketched_ref[:, h:]
    mapping = dot_parts(inverse1, scale * rotation_ref[:h, :], ((0,), (0,)))
    basis = dot_parts(x1, mapping, ((1,), (0,)))
    rest = x2 - dot_parts(x1, ahead, ((1,), (1,)))
    factor(a, upper, inverse)
    mapping = dot_parts(inverse[...], scale * rotation_ref[h:, :], ((0,), (0,)))
    basis_ref[...] = basis + dot_parts(rest, mapping, ((1,), (0,)))
    triangle_ref[:h, :h] = upper1 * (1.0 / scale)
    triangle_ref[:h, h:] = left.T * (1.0 / scale)
    triangle_ref[h:, :h] = jnp.zeros((h, h), F32)
    triangle_ref[h:, h:] = upper[...] * (1.0 / scale)


def basis_and_triangle(side, mine, other, own, sent, rotation, sketched, scale):
    rows, n = sketched.shape
    return pl.pallas_call(
        functools.partial(basis_kernel, scale),
        out_shape=[jax.ShapeDtypeStruct((rows, n), F32), jax.ShapeDtypeStruct((n, n), F32)],
        in_specs=[SMEM] + [VMEM] * 6,
        out_specs=[VMEM] * 2,
        scratch_shapes=[pltpu.VMEM((n // 2, n // 2), F32)] * 3,
        compiler_params=params(),
        cost_estimate=pl.CostEstimate(
            flops=12 * rows * n * n + 40 * n * n * n, bytes_accessed=8 * rows * n + 12 * n * n, transcendentals=n
        ),
    )(side, mine, other, own, sent, rotation, sketched)


def shards(snapshots, sketch, rotation):
    depth = levels("tm")
    cells = snapshots.shape[0] * lax.axis_size("space")
    side = (lax.axis_index("tm").astype(jnp.int32) & 1).reshape(1)

    kept, near = {}, {}
    for mask in range(lax.axis_size("tm") - 2, 0, -2):
        leaving, sketch = sketch_blocks([mask | 1], snapshots, sketch, keep=True)
        near[mask] = partner(leaving, "tm", 0)
        (kept[mask],) = sketch_blocks([mask], snapshots, sketch)
    for level in range(1, depth):
        for mask in [m for m in kept if m >> level & 1]:
            leaving = kept.pop(mask) + near.pop(mask)
            arrived = partner(leaving, "tm", level)
            snapshots, leaving = lax.optimization_barrier((snapshots, leaving))
            if level < depth - 1:
                near[mask ^ 1 << level] = near[mask ^ 1 << level] + arrived
    leaving, kept[0] = sketch_blocks([1, 0], snapshots, sketch)
    near[0] = partner(leaving, "tm", 0)
    sketched, mine, send = gram_halves(side, kept[0], near[0], arrived)
    mine = mine + partner(send, "tm", 0)
    for level in range(1, depth):
        mine = mine + partner(mine, "tm", level)
    for level in range(levels("space")):
        mine = mine + partner(mine, "space", level)
    mine, own = lax.optimization_barrier((mine, first_factor(side, mine)))
    other, sent = partner(mine, "tm", 0), partner(own, "tm", 0)
    return tuple(basis_and_triangle(side, mine, other, own, sent, rotation, sketched, math.sqrt(cells)))


def solution(mesh):
    in_specs = (P("space", "tm"), P("tm", None), P())
    out_specs = (P(("space", "tm"), None), P())
    return jax.shard_map(shards, mesh=mesh, in_specs=in_specs, out_specs=out_specs, check_vma=False)
```

```python
import functools
import math

import jax
import jax.numpy as jnp
from jax import lax
from jax.experimental import pallas as pl
from jax.experimental.pallas import tpu as pltpu
from jax.sharding import PartitionSpec as P

F32, BF16 = jnp.float32, jnp.bfloat16
VMEM = pl.BlockSpec(memory_space=pltpu.VMEM)
SMEM = pl.BlockSpec(memory_space=pltpu.SMEM)
BLOCK = 64
CHUNKS = 2
PANEL = 2


def params(mib=40):
    return pltpu.CompilerParams(vmem_limit_bytes=int(mib * 2**20))


def partner(shard, axis, level):
    return lax.ppermute(shard, axis, [(i, i ^ 1 << level) for i in range(lax.axis_size(axis))])


def levels(axis):
    return lax.axis_size(axis).bit_length() - 1


def split(x):
    high = x.astype(BF16)
    rest = x - high.astype(F32)
    middle = rest.astype(BF16)
    low = (rest - middle.astype(F32)).astype(BF16)
    return high, middle, low


def product(x, y, dims):
    return lax.dot_general(x, y, (dims, ((), ())), preferred_element_type=F32)


LEFT, RIGHT = (0, 0, 1, 0, 1, 2), (0, 1, 0, 2, 1, 0)


def stacked(x, order, axis):
    parts = split(x)
    return jnp.concatenate([parts[i] for i in order], axis=axis)


def dot_parts(x, y, over):
    return product(stacked(x, LEFT, over[0]), stacked(y, RIGHT, over[1]), ((over[0],), (over[1],)))


def sketch_kernel(masks, snapshots_ref, sketch_ref, *rest):
    outs, (tall, wide, arrived, ready) = rest[: len(masks)], rest[len(masks) :]
    rows = tall.shape[0] // len(masks)
    index = lax.axis_index("tm")
    fetch = pltpu.make_async_copy(sketch_ref, wide, ready)
    fetch.start()
    copies = []
    for i, mask in enumerate(masks):
        block = pl.ds(pl.multiple_of((index ^ mask) * rows, rows), rows)
        copies.append(pltpu.make_async_copy(snapshots_ref.at[block], tall.at[pl.ds(rows * i, rows)], arrived.at[i]))
        copies[-1].start()
    fetch.wait()
    for i, out in enumerate(outs):
        copies[i].wait()
        out[...] = jnp.dot(tall[rows * i : rows * (i + 1), :], wide[...], preferred_element_type=F32)


def sketch_blocks(masks, snapshots, sketch):
    rows = snapshots.shape[0] // lax.axis_size("tm")
    depth, columns = sketch.shape
    count = len(masks)
    return pl.pallas_call(
        functools.partial(sketch_kernel, masks),
        out_shape=[jax.ShapeDtypeStruct((rows, columns), F32)] * count,
        in_specs=[pl.BlockSpec(memory_space=pltpu.HBM)] * 2,
        out_specs=[VMEM] * count,
        scratch_shapes=[
            pltpu.VMEM((count * rows, depth), BF16),
            pltpu.VMEM((depth, columns), BF16),
            pltpu.SemaphoreType.DMA((count,)),
            pltpu.SemaphoreType.DMA,
        ],
        compiler_params=params(),
        cost_estimate=pl.CostEstimate(
            flops=2 * count * rows * depth * columns,
            bytes_accessed=count * rows * (2 * depth + 4 * columns) + 2 * depth * columns,
            transcendentals=0,
        ),
    )(pltpu.with_memory_space_constraint(snapshots, pltpu.HBM), pltpu.with_memory_space_constraint(sketch, pltpu.HBM))


def gram_kernel(side_ref, kept_ref, near_ref, far_ref, sketched_ref, keep_ref, send_ref):
    sketched = (kept_ref[...] + near_ref[...]) + far_ref[...]
    sketched_ref[...] = sketched
    high, middle, low = split(sketched)
    rows = ((0,), (0,))
    cross = product(high, middle, rows) + product(high, low, rows)
    gram = product(high, high, rows) + (cross + cross.T + product(middle, middle, rows))
    h = gram.shape[0] // 2
    row = lax.broadcasted_iota(jnp.int32, (h, h), 0)
    column = lax.broadcasted_iota(jnp.int32, (h, h), 1)
    corner = gram[h:, h:]
    diagonal = jnp.sum(jnp.where(row == column, corner, 0.0), axis=0, keepdims=True)
    mixed = jnp.where(row >= column, gram[:h, :h], corner)
    first = side_ref[0] == 0
    keep_ref[:h, :] = jnp.where(first, gram[h:, :h], mixed)
    send_ref[:h, :] = jnp.where(first, mixed, gram[h:, :h])
    keep_ref[h:, :] = jnp.broadcast_to(diagonal, (8, h))
    send_ref[h:, :] = jnp.broadcast_to(diagonal, (8, h))


def gram_halves(side, kept, near, far):
    rows, n = kept.shape
    half = jax.ShapeDtypeStruct((n // 2 + 8, n // 2), F32)
    return pl.pallas_call(
        gram_kernel,
        out_shape=[jax.ShapeDtypeStruct((rows, n), F32), half, half],
        in_specs=[SMEM, VMEM, VMEM, VMEM],
        out_specs=[VMEM] * 3,
        compiler_params=params(),
        cost_estimate=pl.CostEstimate(
            flops=8 * rows * n * n, bytes_accessed=16 * rows * n + 4 * n * n, transcendentals=0
        ),
    )(side, kept, near, far)


def column(v, c):
    return jnp.broadcast_to(v[:, c : c + 1], (8, 128))


def row(v, k):
    return jnp.broadcast_to(v[k : k + 1, :], (8, 128))


def factor(a, upper, inverse):
    n = a.shape[0]
    tiles = n // 128
    lane = lax.broadcasted_iota(jnp.int32, (8, 128), 1)
    sub = lax.broadcasted_iota(jnp.int32, (8, 128), 0)
    groups, width = BLOCK // 8, 8 * PANEL
    zero = jnp.zeros((8, 128), F32)
    for start in range(0, n, BLOCK):
        tile, offset = divmod(start, 128)
        t = []
        for i in range(groups):
            top = start + 8 * i
            t.append([a[top : top + 8, 128 * x : 128 * x + 128] for x in range(tiles)])
            t[i].append(jnp.where(lane == sub + (offset + 8 * i), 1.0, 0.0))
        for q in range(0, groups, PANEL):
            first = offset + 8 * q
            c = {(g, j): column(t[q + g][tile], first + j) for g in range(PANEL) for j in range(8 * g + 8)}
            r, l, m = {}, {}, {}
            pivot = row(c[0, 0], 0)
            for j in range(width):
                r[j] = lax.rsqrt(pivot)
                if j + 1 < width:
                    g, k = divmod(j + 1, 8)
                    m[j + 1, j] = row(c[g, j], k) * r[j]
                    pivot = row(c[g, j + 1], k) - m[j + 1, j] * m[j + 1, j]
                for g in range(j // 8, PANEL):
                    l[g, j] = c[g, j] * r[j]
                for k in range(j + 1, width):
                    if k > j + 1:
                        m[k, j] = row(l[k // 8, j], k % 8)
                    for g in range(k // 8, PANEL):
                        c[g, k] = c[g, k] - l[g, j] * m[k, j]
            p = {}
            for g in range(PANEL):
                mine = t[q + g]
                for j in range(8 * g):
                    mine = [x - l[g, j] * y for x, y in zip(mine, p[j])]
                roots = r[8 * g]
                for jj in range(8):
                    j = 8 * g + jj
                    p[j] = [row(x, jj) * r[j] for x in mine]
                    below = jnp.where(sub > jj, l[g, j], 0.0)
                    mine = [x - below * y for x, y in zip(mine, p[j])]
                    roots = jnp.where(sub == jj, r[j], roots)
                t[q + g] = [x * roots for x in mine]
            for i in range(q + PANEL, groups):
                for g in range(PANEL):
                    c = [column(t[i][tile], first + 8 * g + jj) for jj in range(8)]
                    for jj in range(8):
                        c[jj] = c[jj] * r[8 * g + jj]
                        for kk in range(jj + 1, 8):
                            c[kk] = c[kk] - c[jj] * m[8 * g + kk, 8 * g + jj]
                    for jj in range(8):
                        t[i] = [x - c[jj] * y for x, y in zip(t[i], p[8 * g + jj])]
        done = (lane >= offset) & (lane < offset + BLOCK)
        left, right = [[] for _ in range(tiles)], [[] for _ in range(tiles)]
        for i in range(groups):
            top, own = start + 8 * i, t[i][tiles]
            for x in range(tiles):
                u = w = z = t[i][x]
                if x < tile:
                    u = zero
                elif x > tile:
                    w = zero
                else:
                    u = jnp.where(lane >= sub + (offset + 8 * i), u, 0.0)
                    w = jnp.where(lane < offset, w, own)
                    z = jnp.where(done, own, z)
                upper[top : top + 8, 128 * x : 128 * x + 128] = u
                inverse[top : top + 8, 128 * x : 128 * x + 128] = w
                left[x].append(u)
                right[x].append(z)
        after = start + BLOCK
        if after < n:
            y = jnp.concatenate([jnp.concatenate(v, axis=0) for v in right], axis=1)
            y = stacked(y, RIGHT, 0)
            for x in range(after // 128, tiles):
                update = product(stacked(jnp.concatenate(left[x], axis=0), LEFT, 0), y, ((0,), (0,)))
                for top in range(max(after, 128 * x), 128 * x + 128, 8):
                    for k in range(tiles):
                        old = a[top : top + 8, 128 * k : 128 * k + 128]
                        if k == tile:
                            old = jnp.where(done, 0.0, old)
                        new = update[top - 128 * x : top - 128 * x + 8, 128 * k : 128 * k + 128]
                        a[top : top + 8, 128 * k : 128 * k + 128] = old - new


def triangles(shape):
    row = lax.broadcasted_iota(jnp.int32, shape, 0)
    column = lax.broadcasted_iota(jnp.int32, shape, 1)
    return row > column, row == column


def first_kernel(side_ref, mine_ref, out_ref, a, upper, inverse):
    h = a.shape[0]
    lower, middle = triangles((h, h))

    @pl.when(side_ref[0] == 1)
    def _():
        mixed = mine_ref[:h, :]
        flipped = mixed.T
        a[...] = jnp.where(lower | middle, mixed, flipped)
        out_ref[:h, :] = jnp.where(lower, flipped, jnp.where(middle, mine_ref[h : h + 1, :], mixed))
        factor(a, upper, inverse)
        out_ref[h : 2 * h, :] = jnp.where(lower | middle, inverse[...], upper[...])
        diagonal = jnp.sum(jnp.where(middle, upper[...], 0.0), axis=0, keepdims=True)
        out_ref[2 * h :, :] = jnp.broadcast_to(diagonal, (8, h))

    @pl.when(side_ref[0] == 0)
    def _():
        out_ref[:h, :] = mine_ref[:h, :]
        out_ref[h:, :] = jnp.zeros((h + 8, h), F32)


def first_factor(side, mine):
    h = mine.shape[1]
    return pl.pallas_call(
        first_kernel,
        out_shape=jax.ShapeDtypeStruct((2 * h + 8, h), F32),
        in_specs=[SMEM, VMEM],
        out_specs=VMEM,
        scratch_shapes=[pltpu.VMEM((h, h), F32)] * 3,
        compiler_params=params(),
        cost_estimate=pl.CostEstimate(flops=10 * h * h * h, bytes_accessed=8 * h * h, transcendentals=h),
    )(side, mine)


def basis_kernel(
    scale, side_ref, own_ref, sent_ref, rotation_ref, sketched_ref, basis_ref, triangle_ref, a, upper, inverse, rest, basis, triangle, sent
):
    h = a.shape[0]
    rows = basis.shape[0]
    lower, middle = triangles((h, h))
    first = side_ref[0] == 0
    below = jnp.where(first, own_ref[:h, :], sent_ref[:h, :])
    corner = jnp.where(first, sent_ref[:h, :], own_ref[:h, :])
    factors = jnp.where(first, sent_ref[h:, :], own_ref[h:, :])
    inverse1 = jnp.where(lower | middle, factors[:h, :], 0.0)
    upper1 = jnp.where(lower, 0.0, jnp.where(middle, factors[h : h + 1, :], factors[:h, :]))
    left = dot_parts(below, inverse1, (1, 1))
    a[...] = corner - dot_parts(left, left, (1, 1))
    ahead = dot_parts(left, inverse1, (1, 0))
    triangle[:h, :h] = upper1 * (1.0 / scale)
    triangle[:h, h:] = left.T * (1.0 / scale)
    triangle[h:, :h] = jnp.zeros((h, h), F32)
    copies = [pltpu.make_async_copy(triangle.at[pl.ds(h * i, h)], triangle_ref.at[pl.ds(h * i, h)], sent.at[i]) for i in range(2)]
    copies[0].start()
    x1, x2 = sketched_ref[:, :h], sketched_ref[:, h:]
    mapping = dot_parts(inverse1, scale * rotation_ref[:h, :], (0, 0))
    basis[...] = dot_parts(x1, mapping, (1, 0))
    rest[...] = stacked(x2 - dot_parts(x1, ahead, (1, 1)), LEFT, 1)
    turned = stacked(scale * rotation_ref[h:, :], RIGHT, 0)
    factor(a, upper, inverse)
    triangle[h:, h:] = upper[...] * (1.0 / scale)
    copies[1].start()
    mapping = stacked(product(stacked(inverse[...], LEFT, 0), turned, ((0,), (0,))), RIGHT, 0)
    step = rows // CHUNKS
    for i in range(CHUNKS):
        part = pl.ds(step * i, step)
        basis[part, :] += product(rest[part, :], mapping, ((1,), (0,)))
        copies.append(pltpu.make_async_copy(basis.at[part], basis_ref.at[part], sent.at[2 + i]))
        copies[-1].start()
    for copy in copies:
        copy.wait()


def basis_and_triangle(side, own, sent, rotation, sketched, scale):
    rows, n = sketched.shape
    h = n // 2
    return pl.pallas_call(
        functools.partial(basis_kernel, scale),
        out_shape=[jax.ShapeDtypeStruct((rows, n), F32), jax.ShapeDtypeStruct((n, n), F32)],
        in_specs=[SMEM] + [VMEM] * 4,
        out_specs=[pl.BlockSpec(memory_space=pltpu.HBM)] * 2,
        scratch_shapes=[pltpu.VMEM((h, h), F32)] * 3
        + [
            pltpu.VMEM((rows, len(LEFT) * h), BF16),
            pltpu.VMEM((rows, n), F32),
            pltpu.VMEM((n, n), F32),
            pltpu.SemaphoreType.DMA((2 + CHUNKS,)),
        ],
        compiler_params=params(),
        cost_estimate=pl.CostEstimate(
            flops=12 * rows * n * n + 40 * n * n * n, bytes_accessed=8 * rows * n + 12 * n * n, transcendentals=n
        ),
    )(side, own, sent, rotation, sketched)


def shards(snapshots, sketch, rotation):
    depth = levels("tm")
    cells = snapshots.shape[0] * lax.axis_size("space")
    side = (lax.axis_index("tm").astype(jnp.int32) & 1).reshape(1)

    kept, near = {}, {}
    for mask in range(lax.axis_size("tm") - 2, 0, -2):
        (leaving,) = sketch_blocks([mask | 1], snapshots, sketch)
        near[mask] = partner(leaving, "tm", 0)
        (kept[mask],) = sketch_blocks([mask], snapshots, sketch)
    for level in range(1, depth):
        for mask in [m for m in kept if m >> level & 1]:
            leaving = kept.pop(mask) + near.pop(mask)
            arrived = partner(leaving, "tm", level)
            snapshots, leaving = lax.optimization_barrier((snapshots, leaving))
            if level < depth - 1:
                near[mask ^ 1 << level] = near[mask ^ 1 << level] + arrived
    leaving, kept[0] = sketch_blocks([1, 0], snapshots, sketch)
    near[0] = partner(leaving, "tm", 0)
    sketched, mine, send = gram_halves(side, kept[0], near[0], arrived)
    mine = mine + partner(send, "tm", 0)
    for level in range(1, depth):
        mine = mine + partner(mine, "tm", level)
    for level in range(levels("space")):
        mine = mine + partner(mine, "space", level)
    own = first_factor(side, mine)
    return tuple(basis_and_triangle(side, own, partner(own, "tm", 0), rotation, sketched, math.sqrt(cells)))


def solution(mesh):
    in_specs = (P("space", "tm"), P("tm", None), P())
    out_specs = (P(("space", "tm"), None), P())
    return jax.shard_map(shards, mesh=mesh, in_specs=in_specs, out_specs=out_specs, check_vma=False)
```

```python
import functools
import math

import jax
import jax.numpy as jnp
from jax import lax
from jax.experimental import pallas as pl
from jax.experimental.pallas import tpu as pltpu
from jax.sharding import PartitionSpec as P

F32, BF16 = jnp.float32, jnp.bfloat16
VMEM = pl.BlockSpec(memory_space=pltpu.VMEM)
SMEM = pl.BlockSpec(memory_space=pltpu.SMEM)
BLOCK = 64
CHUNKS = 4
PANEL = 2


def params(mib=40):
    return pltpu.CompilerParams(vmem_limit_bytes=int(mib * 2**20))


AXES = ("space", "tm")


def partner(shard, flip):
    count = lax.axis_size("space") * lax.axis_size("tm")
    return lax.ppermute(shard, AXES, [(i, i ^ flip) for i in range(count)])


def levels(axis):
    return lax.axis_size(axis).bit_length() - 1


def split(x):
    high = x.astype(BF16)
    rest = x - high.astype(F32)
    middle = rest.astype(BF16)
    low = (rest - middle.astype(F32)).astype(BF16)
    return high, middle, low


def product(x, y, dims):
    return lax.dot_general(x, y, (dims, ((), ())), preferred_element_type=F32)


LEFT, RIGHT = (0, 0, 1, 0, 1, 2), (0, 1, 0, 2, 1, 0)


def stacked(x, order, axis):
    parts = split(x)
    return jnp.concatenate([parts[i] for i in order], axis=axis)


def dot_parts(x, y, over):
    return product(stacked(x, LEFT, over[0]), stacked(y, RIGHT, over[1]), ((over[0],), (over[1],)))


def sketch_kernel(masks, snapshots_ref, sketch_ref, *rest):
    outs, (tall, wide, arrived, ready) = rest[: len(masks)], rest[len(masks) :]
    rows = tall.shape[0] // len(masks)
    index = lax.axis_index("tm")
    fetch = pltpu.make_async_copy(sketch_ref, wide, ready)
    fetch.start()
    copies = []
    for i, mask in enumerate(masks):
        block = pl.ds(pl.multiple_of((index ^ mask) * rows, rows), rows)
        copies.append(pltpu.make_async_copy(snapshots_ref.at[block], tall.at[pl.ds(rows * i, rows)], arrived.at[i]))
        copies[-1].start()
    fetch.wait()
    for i, out in enumerate(outs):
        copies[i].wait()
        out[...] = jnp.dot(tall[rows * i : rows * (i + 1), :], wide[...], preferred_element_type=F32)


def sketch_blocks(masks, snapshots, sketch):
    rows = snapshots.shape[0] // lax.axis_size("tm")
    depth, columns = sketch.shape
    count = len(masks)
    return pl.pallas_call(
        functools.partial(sketch_kernel, masks),
        out_shape=[jax.ShapeDtypeStruct((rows, columns), F32)] * count,
        in_specs=[pl.BlockSpec(memory_space=pltpu.HBM)] * 2,
        out_specs=[VMEM] * count,
        scratch_shapes=[
            pltpu.VMEM((count * rows, depth), BF16),
            pltpu.VMEM((depth, columns), BF16),
            pltpu.SemaphoreType.DMA((count,)),
            pltpu.SemaphoreType.DMA,
        ],
        compiler_params=params(),
        cost_estimate=pl.CostEstimate(
            flops=2 * count * rows * depth * columns,
            bytes_accessed=count * rows * (2 * depth + 4 * columns) + 2 * depth * columns,
            transcendentals=0,
        ),
    )(pltpu.with_memory_space_constraint(snapshots, pltpu.HBM), pltpu.with_memory_space_constraint(sketch, pltpu.HBM))


def gram_kernel(side_ref, kept_ref, near_ref, far_ref, sketched_ref, keep_ref, send_ref):
    sketched = (kept_ref[...] + near_ref[...]) + far_ref[...]
    sketched_ref[...] = sketched
    high, middle, low = split(sketched)
    rows = ((0,), (0,))
    cross = product(high, middle, rows) + product(high, low, rows)
    gram = product(high, high, rows) + (cross + cross.T + product(middle, middle, rows))
    h = gram.shape[0] // 2
    row = lax.broadcasted_iota(jnp.int32, (h, h), 0)
    column = lax.broadcasted_iota(jnp.int32, (h, h), 1)
    corner = gram[h:, h:]
    diagonal = jnp.sum(jnp.where(row == column, corner, 0.0), axis=0, keepdims=True)
    mixed = jnp.where(row >= column, gram[:h, :h], corner)
    first = side_ref[0] == 0
    keep_ref[:h, :] = jnp.where(first, gram[h:, :h], mixed)
    send_ref[:h, :] = jnp.where(first, mixed, gram[h:, :h])
    keep_ref[h:, :] = jnp.broadcast_to(diagonal, (8, h))
    send_ref[h:, :] = jnp.broadcast_to(diagonal, (8, h))


def gram_halves(side, kept, near, far):
    rows, n = kept.shape
    half = jax.ShapeDtypeStruct((n // 2 + 8, n // 2), F32)
    return pl.pallas_call(
        gram_kernel,
        out_shape=[jax.ShapeDtypeStruct((rows, n), F32), half, half],
        in_specs=[SMEM, VMEM, VMEM, VMEM],
        out_specs=[VMEM] * 3,
        compiler_params=params(),
        cost_estimate=pl.CostEstimate(
            flops=8 * rows * n * n, bytes_accessed=16 * rows * n + 4 * n * n, transcendentals=0
        ),
    )(side, kept, near, far)


def column(v, c):
    return jnp.broadcast_to(v[:, c : c + 1], (8, 128))


def row(v, k):
    return jnp.broadcast_to(v[k : k + 1, :], (8, 128))


def factor(a, upper, inverse):
    n = a.shape[0]
    tiles = n // 128
    lane = lax.broadcasted_iota(jnp.int32, (8, 128), 1)
    sub = lax.broadcasted_iota(jnp.int32, (8, 128), 0)
    groups, width = BLOCK // 8, 8 * PANEL
    zero = jnp.zeros((8, 128), F32)
    for start in range(0, n, BLOCK):
        tile, offset = divmod(start, 128)
        t = []
        for i in range(groups):
            top = start + 8 * i
            t.append([a[top : top + 8, 128 * x : 128 * x + 128] for x in range(tiles)])
            t[i].append(jnp.where(lane == sub + (offset + 8 * i), 1.0, 0.0))
        for q in range(0, groups, PANEL):
            first = offset + 8 * q
            c = {(g, j): column(t[q + g][tile], first + j) for g in range(PANEL) for j in range(8 * g + 8)}
            r, l, m = {}, {}, {}
            pivot = row(c[0, 0], 0)
            for j in range(width):
                r[j] = lax.rsqrt(pivot)
                if j + 1 < width:
                    g, k = divmod(j + 1, 8)
                    m[j + 1, j] = row(c[g, j], k) * r[j]
                    pivot = row(c[g, j + 1], k) - m[j + 1, j] * m[j + 1, j]
                for g in range(j // 8, PANEL):
                    l[g, j] = c[g, j] * r[j]
                for k in range(j + 1, width):
                    if k > j + 1:
                        m[k, j] = row(l[k // 8, j], k % 8)
                    for g in range(k // 8, PANEL):
                        c[g, k] = c[g, k] - l[g, j] * m[k, j]
            p = {}
            for g in range(PANEL):
                mine = t[q + g]
                for j in range(8 * g):
                    mine = [x - l[g, j] * y for x, y in zip(mine, p[j])]
                roots = r[8 * g]
                for jj in range(8):
                    j = 8 * g + jj
                    p[j] = [row(x, jj) * r[j] for x in mine]
                    below = jnp.where(sub > jj, l[g, j], 0.0)
                    mine = [x - below * y for x, y in zip(mine, p[j])]
                    roots = jnp.where(sub == jj, r[j], roots)
                t[q + g] = [x * roots for x in mine]
            for i in range(q + PANEL, groups):
                for g in range(PANEL):
                    c = [column(t[i][tile], first + 8 * g + jj) for jj in range(8)]
                    for jj in range(8):
                        c[jj] = c[jj] * r[8 * g + jj]
                        for kk in range(jj + 1, 8):
                            c[kk] = c[kk] - c[jj] * m[8 * g + kk, 8 * g + jj]
                    for jj in range(8):
                        t[i] = [x - c[jj] * y for x, y in zip(t[i], p[8 * g + jj])]
        done = (lane >= offset) & (lane < offset + BLOCK)
        left, right = [[] for _ in range(tiles)], [[] for _ in range(tiles)]
        for i in range(groups):
            top, own = start + 8 * i, t[i][tiles]
            for x in range(tiles):
                u = w = z = t[i][x]
                if x < tile:
                    u = zero
                elif x > tile:
                    w = zero
                else:
                    u = jnp.where(lane >= sub + (offset + 8 * i), u, 0.0)
                    w = jnp.where(lane < offset, w, own)
                    z = jnp.where(done, own, z)
                upper[top : top + 8, 128 * x : 128 * x + 128] = u
                inverse[top : top + 8, 128 * x : 128 * x + 128] = w
                left[x].append(u)
                right[x].append(z)
        after = start + BLOCK
        if after < n:
            y = jnp.concatenate([jnp.concatenate(v, axis=0) for v in right], axis=1)
            y = stacked(y, RIGHT, 0)
            for x in range(after // 128, tiles):
                update = product(stacked(jnp.concatenate(left[x], axis=0), LEFT, 0), y, ((0,), (0,)))
                for top in range(max(after, 128 * x), 128 * x + 128, 8):
                    for k in range(tiles):
                        old = a[top : top + 8, 128 * k : 128 * k + 128]
                        if k == tile:
                            old = jnp.where(done, 0.0, old)
                        new = update[top - 128 * x : top - 128 * x + 8, 128 * k : 128 * k + 128]
                        a[top : top + 8, 128 * k : 128 * k + 128] = old - new


def triangles(shape):
    row = lax.broadcasted_iota(jnp.int32, shape, 0)
    column = lax.broadcasted_iota(jnp.int32, shape, 1)
    return row > column, row == column


def first_kernel(side_ref, mine_ref, out_ref, a, upper, inverse):
    h = a.shape[0]
    lower, middle = triangles((h, h))

    @pl.when(side_ref[0] == 1)
    def _():
        mixed = mine_ref[:h, :]
        flipped = mixed.T
        a[...] = jnp.where(lower | middle, mixed, flipped)
        out_ref[:h, :] = jnp.where(lower, flipped, jnp.where(middle, mine_ref[h : h + 1, :], mixed))
        factor(a, upper, inverse)
        out_ref[h : 2 * h, :] = jnp.where(lower | middle, inverse[...], upper[...])
        diagonal = jnp.sum(jnp.where(middle, upper[...], 0.0), axis=0, keepdims=True)
        out_ref[2 * h :, :] = jnp.broadcast_to(diagonal, (8, h))

    @pl.when(side_ref[0] == 0)
    def _():
        out_ref[:h, :] = mine_ref[:h, :]
        out_ref[h:, :] = jnp.zeros((h + 8, h), F32)


def first_factor(side, mine):
    h = mine.shape[1]
    return pl.pallas_call(
        first_kernel,
        out_shape=jax.ShapeDtypeStruct((2 * h + 8, h), F32),
        in_specs=[SMEM, VMEM],
        out_specs=VMEM,
        scratch_shapes=[pltpu.VMEM((h, h), F32)] * 3,
        compiler_params=params(),
        cost_estimate=pl.CostEstimate(flops=10 * h * h * h, bytes_accessed=8 * h * h, transcendentals=h),
    )(side, mine)


def basis_kernel(
    scale, side_ref, own_ref, sent_ref, rotation_ref, sketched_ref, basis_ref, triangle_ref, a, upper, inverse, rest, basis, triangle, sent
):
    h = a.shape[0]
    rows = basis.shape[0]
    lower, middle = triangles((h, h))
    first = side_ref[0] == 0
    below = jnp.where(first, own_ref[:h, :], sent_ref[:h, :])
    corner = jnp.where(first, sent_ref[:h, :], own_ref[:h, :])
    factors = jnp.where(first, sent_ref[h:, :], own_ref[h:, :])
    inverse1 = jnp.where(lower | middle, factors[:h, :], 0.0)
    upper1 = jnp.where(lower, 0.0, jnp.where(middle, factors[h : h + 1, :], factors[:h, :]))
    left = dot_parts(below, inverse1, (1, 1))
    a[...] = corner - dot_parts(left, left, (1, 1))
    ahead = dot_parts(left, inverse1, (1, 0))
    triangle[:h, :h] = upper1 * (1.0 / scale)
    triangle[:h, h:] = left.T * (1.0 / scale)
    triangle[h:, :h] = jnp.zeros((h, h), F32)
    copies = [pltpu.make_async_copy(triangle.at[pl.ds(h * i, h)], triangle_ref.at[pl.ds(h * i, h)], sent.at[i]) for i in range(2)]
    copies[0].start()
    x1, x2 = sketched_ref[:, :h], sketched_ref[:, h:]
    mapping = dot_parts(inverse1, scale * rotation_ref[:h, :], (0, 0))
    basis[...] = dot_parts(x1, mapping, (1, 0))
    rest[...] = stacked(x2 - dot_parts(x1, ahead, (1, 1)), LEFT, 1)
    turned = stacked(scale * rotation_ref[h:, :], RIGHT, 0)
    factor(a, upper, inverse)
    triangle[h:, h:] = upper[...] * (1.0 / scale)
    copies[1].start()
    mapping = stacked(product(stacked(inverse[...], LEFT, 0), turned, ((0,), (0,))), RIGHT, 0)
    step = rows // CHUNKS
    for i in range(CHUNKS):
        part = pl.ds(step * i, step)
        basis[part, :] += product(rest[part, :], mapping, ((1,), (0,)))
        copies.append(pltpu.make_async_copy(basis.at[part], basis_ref.at[part], sent.at[2 + i]))
        copies[-1].start()
    for copy in copies:
        copy.wait()


def basis_and_triangle(side, own, sent, rotation, sketched, scale):
    rows, n = sketched.shape
    h = n // 2
    return pl.pallas_call(
        functools.partial(basis_kernel, scale),
        out_shape=[jax.ShapeDtypeStruct((rows, n), F32), jax.ShapeDtypeStruct((n, n), F32)],
        in_specs=[SMEM] + [VMEM] * 4,
        out_specs=[pl.BlockSpec(memory_space=pltpu.HBM)] * 2,
        scratch_shapes=[pltpu.VMEM((h, h), F32)] * 3
        + [
            pltpu.VMEM((rows, len(LEFT) * h), BF16),
            pltpu.VMEM((rows, n), F32),
            pltpu.VMEM((n, n), F32),
            pltpu.SemaphoreType.DMA((2 + CHUNKS,)),
        ],
        compiler_params=params(),
        cost_estimate=pl.CostEstimate(
            flops=12 * rows * n * n + 40 * n * n * n, bytes_accessed=8 * rows * n + 12 * n * n, transcendentals=n
        ),
    )(side, own, sent, rotation, sketched)


def shards(snapshots, sketch, rotation):
    depth = levels("tm")
    cells = snapshots.shape[0] * lax.axis_size("space")
    side = (lax.axis_index("tm").astype(jnp.int32) & 1).reshape(1)

    kept, near = {}, {}
    for mask in range(lax.axis_size("tm") - 2, 0, -2):
        (leaving,) = sketch_blocks([mask | 1], snapshots, sketch)
        near[mask] = partner(leaving, 1)
        (kept[mask],) = sketch_blocks([mask], snapshots, sketch)
    for level in range(1, depth):
        for mask in [m for m in kept if m >> level & 1]:
            leaving = kept.pop(mask) + near.pop(mask)
            arrived = partner(leaving, 1 << level)
            snapshots, leaving = lax.optimization_barrier((snapshots, leaving))
            if level < depth - 1:
                near[mask ^ 1 << level] = near[mask ^ 1 << level] + arrived
    leaving, kept[0] = sketch_blocks([1, 0], snapshots, sketch)
    near[0] = partner(leaving, 1)
    sketched, mine, send = gram_halves(side, kept[0], near[0], arrived)
    mine = mine + partner(send, 1)
    flips = [1 << level for level in range(1, depth + levels("space"))]
    if len(flips) > 1:
        x, y, *flips = flips
        mine = mine + ((partner(mine, x | y) + partner(mine, x)) + partner(mine, y))
    for flip in flips:
        mine = mine + partner(mine, flip)
    own = first_factor(side, mine)
    return tuple(basis_and_triangle(side, own, partner(own, 1), rotation, sketched, math.sqrt(cells)))


def solution(mesh):
    in_specs = (P("space", "tm"), P("tm", None), P())
    out_specs = (P(("space", "tm"), None), P())
    return jax.shard_map(shards, mesh=mesh, in_specs=in_specs, out_specs=out_specs, check_vma=False)
```

```python
import functools
import math

import jax
import jax.numpy as jnp
from jax import lax
from jax.experimental import pallas as pl
from jax.experimental.pallas import tpu as pltpu
from jax.sharding import PartitionSpec as P

F32, BF16 = jnp.float32, jnp.bfloat16
VMEM = pl.BlockSpec(memory_space=pltpu.VMEM)
SMEM = pl.BlockSpec(memory_space=pltpu.SMEM)
BLOCK = 64
SLICES = 4
PARTS = 2
CHUNKS = 4
PANEL = 2


def params(mib=40):
    return pltpu.CompilerParams(vmem_limit_bytes=int(mib * 2**20))


AXES = ("space", "tm")


def partner(shard, flip):
    count = lax.axis_size("space") * lax.axis_size("tm")
    return lax.ppermute(shard, AXES, [(i, i ^ flip) for i in range(count)])


def levels(axis):
    return lax.axis_size(axis).bit_length() - 1


def split(x):
    high = x.astype(BF16)
    rest = x - high.astype(F32)
    middle = rest.astype(BF16)
    low = (rest - middle.astype(F32)).astype(BF16)
    return high, middle, low


def product(x, y, dims):
    return lax.dot_general(x, y, (dims, ((), ())), preferred_element_type=F32)


LEFT, RIGHT = (0, 0, 1, 0, 1, 2), (0, 1, 0, 2, 1, 0)


def stacked(x, order, axis):
    parts = split(x)
    return jnp.concatenate([parts[i] for i in order], axis=axis)


def dot_parts(x, y, over):
    return product(stacked(x, LEFT, over[0]), stacked(y, RIGHT, over[1]), ((over[0],), (over[1],)))


def triangles(shape):
    row = lax.broadcasted_iota(jnp.int32, shape, 0)
    column = lax.broadcasted_iota(jnp.int32, shape, 1)
    return row > column, row == column


def rows_of(ref, mask, rows):
    block = lax.axis_index("tm") ^ mask
    return ref.at[pl.ds(pl.multiple_of(block * rows, rows), rows)]


def in_hbm(x):
    return pltpu.with_memory_space_constraint(x, pltpu.HBM)


def leaving_kernel(leaves, stays, snapshots_ref, sketch_ref, *rest):
    *outs, next_ref, wide, tall, arrived = rest
    rows, step = tall.shape[0], outs[0].shape[0]
    copies = [
        pltpu.make_async_copy(sketch_ref, wide, arrived.at[0]),
        pltpu.make_async_copy(rows_of(snapshots_ref, leaves, rows), tall, arrived.at[1]),
        pltpu.make_async_copy(rows_of(snapshots_ref, stays, rows), next_ref, arrived.at[2]),
    ]
    for copy in copies:
        copy.start()
    copies[0].wait()
    copies[1].wait()
    for i, out in enumerate(outs):
        out[...] = jnp.dot(tall[step * i : step * (i + 1), :], wide[...], preferred_element_type=F32)
    copies[2].wait()


def sketch_leaving(leaves, stays, snapshots, sketch):
    rows = snapshots.shape[0] // lax.axis_size("tm")
    depth, columns = sketch.shape
    return pl.pallas_call(
        functools.partial(leaving_kernel, leaves, stays),
        out_shape=[jax.ShapeDtypeStruct((rows // PARTS, columns), F32)] * PARTS
        + [jax.ShapeDtypeStruct((rows, depth), BF16), jax.ShapeDtypeStruct((depth, columns), BF16)],
        in_specs=[pl.BlockSpec(memory_space=pltpu.HBM)] * 2,
        out_specs=[VMEM] * (PARTS + 2),
        scratch_shapes=[pltpu.VMEM((rows, depth), BF16), pltpu.SemaphoreType.DMA((3,))],
        compiler_params=params(),
        cost_estimate=pl.CostEstimate(
            flops=2 * rows * depth * columns, bytes_accessed=4 * rows * depth + 4 * depth * columns, transcendentals=0
        ),
    )(in_hbm(snapshots), in_hbm(sketch))


def staying_kernel(rows_ref, sketch_ref, *outs):
    step = outs[0].shape[0]
    for i, out in enumerate(outs):
        out[...] = jnp.dot(rows_ref[step * i : step * (i + 1), :], sketch_ref[...], preferred_element_type=F32)


def sketch_staying(rows, sketch):
    count, depth = rows.shape
    columns = sketch.shape[1]
    return pl.pallas_call(
        staying_kernel,
        out_shape=[jax.ShapeDtypeStruct((count // PARTS, columns), F32)] * PARTS,
        in_specs=[VMEM] * 2,
        out_specs=[VMEM] * PARTS,
        compiler_params=params(),
        cost_estimate=pl.CostEstimate(flops=2 * count * depth * columns, bytes_accessed=2 * count * depth, transcendentals=0),
    )(rows, sketch)


def last_kernel(snapshots_ref, sketch_ref, *refs):
    *outs, tall, wide, arrived = refs
    rows = tall.shape[0] // 2
    copies = [pltpu.make_async_copy(sketch_ref, wide, arrived.at[0])]
    for i in range(2):
        copies.append(pltpu.make_async_copy(rows_of(snapshots_ref, 1 - i, rows), tall.at[pl.ds(rows * i, rows)], arrived.at[1 + i]))
    for copy in copies:
        copy.start()
    copies[0].wait()
    place = 0
    for i, out in enumerate(outs):
        if i in (0, SLICES):
            copies[1 + i // SLICES].wait()
        count = out.shape[0]
        out[...] = jnp.dot(tall[place : place + count, :], wide[...], preferred_element_type=F32)
        place += count


def sketch_last(snapshots, sketch):
    rows = snapshots.shape[0] // lax.axis_size("tm")
    depth, columns = sketch.shape
    return pl.pallas_call(
        last_kernel,
        out_shape=[jax.ShapeDtypeStruct((rows // SLICES, columns), F32)] * SLICES + [jax.ShapeDtypeStruct((rows, columns), F32)],
        in_specs=[pl.BlockSpec(memory_space=pltpu.HBM)] * 2,
        out_specs=[VMEM] * (SLICES + 1),
        scratch_shapes=[
            pltpu.VMEM((2 * rows, depth), BF16),
            pltpu.VMEM((depth, columns), BF16),
            pltpu.SemaphoreType.DMA((3,)),
        ],
        compiler_params=params(),
        cost_estimate=pl.CostEstimate(flops=1, bytes_accessed=1, transcendentals=0),
    )(in_hbm(snapshots), in_hbm(sketch))


def gram_kernel(part, side_ref, kept_ref, far_ref, *rest):
    near_refs, rest = rest[: SLICES // PARTS], rest[SLICES // PARTS :]
    before, (sketched_ref, *outs) = rest[: min(part, 1)], rest[min(part, 1) :]
    rows = far_ref.shape[0]
    mine = slice(rows * part, rows * (part + 1))
    sketched = (kept_ref[mine, :] + jnp.concatenate([ref[...] for ref in near_refs], axis=0)) + far_ref[...]
    sketched_ref[...] = sketched
    gram = dot_parts(sketched, sketched, (0, 0))
    if before:
        gram = gram + before[0][...]
    if part < PARTS - 1:
        outs[0][...] = gram
        return
    keep_ref, send_ref = outs
    h = gram.shape[0] // 2
    lower, middle = triangles((h, h))
    corner = gram[h:, h:]
    diagonal = jnp.sum(jnp.where(middle, corner, 0.0), axis=0, keepdims=True)
    mixed = jnp.where(lower | middle, gram[:h, :h], corner)
    first = side_ref[0] == 0
    keep_ref[:h, :] = jnp.where(first, gram[h:, :h], mixed)
    send_ref[:h, :] = jnp.where(first, mixed, gram[h:, :h])
    keep_ref[h:, :] = jnp.broadcast_to(diagonal, (8, h))
    send_ref[h:, :] = jnp.broadcast_to(diagonal, (8, h))


def gram_part(part, side, kept, near, far, *before):
    rows, n = far.shape
    half = jax.ShapeDtypeStruct((n // 2 + 8, n // 2), F32)
    outs = [half, half] if part == PARTS - 1 else [jax.ShapeDtypeStruct((n, n), F32)]
    return pl.pallas_call(
        functools.partial(gram_kernel, part),
        out_shape=[jax.ShapeDtypeStruct((rows, n), F32)] + outs,
        in_specs=[SMEM] + [VMEM] * (2 + len(near) + len(before)),
        out_specs=[VMEM] * (1 + len(outs)),
        compiler_params=params(),
        cost_estimate=pl.CostEstimate(
            flops=12 * rows * n * n, bytes_accessed=16 * rows * n + 4 * n * n, transcendentals=0
        ),
    )(side, kept, far, *near, *before)


def column(v, c):
    return jnp.broadcast_to(v[:, c : c + 1], (8, 128))


def row(v, k):
    return jnp.broadcast_to(v[k : k + 1, :], (8, 128))


def factor(a, upper, inverse):
    n = a.shape[0]
    tiles = n // 128
    lane = lax.broadcasted_iota(jnp.int32, (8, 128), 1)
    sub = lax.broadcasted_iota(jnp.int32, (8, 128), 0)
    groups, width = BLOCK // 8, 8 * PANEL
    zero = jnp.zeros((8, 128), F32)
    for start in range(0, n, BLOCK):
        tile, offset = divmod(start, 128)
        t = []
        for i in range(groups):
            top = start + 8 * i
            t.append([a[top : top + 8, 128 * x : 128 * x + 128] for x in range(tiles)])
            t[i].append(jnp.where(lane == sub + (offset + 8 * i), 1.0, 0.0))
        for q in range(0, groups, PANEL):
            first = offset + 8 * q
            c = {(g, j): column(t[q + g][tile], first + j) for g in range(PANEL) for j in range(8 * g + 8)}
            r, l, m = {}, {}, {}
            pivot = row(c[0, 0], 0)
            for j in range(width):
                r[j] = lax.rsqrt(pivot)
                if j + 1 < width:
                    g, k = divmod(j + 1, 8)
                    m[j + 1, j] = row(c[g, j], k) * r[j]
                    pivot = row(c[g, j + 1], k) - m[j + 1, j] * m[j + 1, j]
                for g in range(j // 8, PANEL):
                    l[g, j] = c[g, j] * r[j]
                for k in range(j + 1, width):
                    if k > j + 1:
                        m[k, j] = row(l[k // 8, j], k % 8)
                    for g in range(k // 8, PANEL):
                        c[g, k] = c[g, k] - l[g, j] * m[k, j]
            p = {}
            for g in range(PANEL):
                mine = t[q + g]
                for j in range(8 * g):
                    mine = [x - l[g, j] * y for x, y in zip(mine, p[j])]
                roots = r[8 * g]
                for jj in range(8):
                    j = 8 * g + jj
                    p[j] = [row(x, jj) * r[j] for x in mine]
                    below = jnp.where(sub > jj, l[g, j], 0.0)
                    mine = [x - below * y for x, y in zip(mine, p[j])]
                    roots = jnp.where(sub == jj, r[j], roots)
                t[q + g] = [x * roots for x in mine]
            for i in range(q + PANEL, groups):
                for g in range(PANEL):
                    c = [column(t[i][tile], first + 8 * g + jj) for jj in range(8)]
                    for jj in range(8):
                        c[jj] = c[jj] * r[8 * g + jj]
                        for kk in range(jj + 1, 8):
                            c[kk] = c[kk] - c[jj] * m[8 * g + kk, 8 * g + jj]
                    for jj in range(8):
                        t[i] = [x - c[jj] * y for x, y in zip(t[i], p[8 * g + jj])]
        done = (lane >= offset) & (lane < offset + BLOCK)
        left, right = [[] for _ in range(tiles)], [[] for _ in range(tiles)]
        for i in range(groups):
            top, own = start + 8 * i, t[i][tiles]
            for x in range(tiles):
                u = w = z = t[i][x]
                if x < tile:
                    u = zero
                elif x > tile:
                    w = zero
                else:
                    u = jnp.where(lane >= sub + (offset + 8 * i), u, 0.0)
                    w = jnp.where(lane < offset, w, own)
                    z = jnp.where(done, own, z)
                upper[top : top + 8, 128 * x : 128 * x + 128] = u
                inverse[top : top + 8, 128 * x : 128 * x + 128] = w
                left[x].append(u)
                right[x].append(z)
        after = start + BLOCK
        if after < n:
            y = jnp.concatenate([jnp.concatenate(v, axis=0) for v in right], axis=1)
            y = stacked(y, RIGHT, 0)
            for x in range(after // 128, tiles):
                update = product(stacked(jnp.concatenate(left[x], axis=0), LEFT, 0), y, ((0,), (0,)))
                for top in range(max(after, 128 * x), 128 * x + 128, 8):
                    for k in range(tiles):
                        old = a[top : top + 8, 128 * k : 128 * k + 128]
                        if k == tile:
                            old = jnp.where(done, 0.0, old)
                        new = update[top - 128 * x : top - 128 * x + 8, 128 * k : 128 * k + 128]
                        a[top : top + 8, 128 * k : 128 * k + 128] = old - new


def first_kernel(side_ref, mine_ref, out_ref, a, upper, inverse):
    h = a.shape[0]
    lower, middle = triangles((h, h))

    @pl.when(side_ref[0] == 1)
    def _():
        mixed = mine_ref[:h, :]
        flipped = mixed.T
        a[...] = jnp.where(lower | middle, mixed, flipped)
        out_ref[:h, :] = jnp.where(lower, flipped, jnp.where(middle, mine_ref[h : h + 1, :], mixed))
        factor(a, upper, inverse)
        out_ref[h : 2 * h, :] = jnp.where(lower | middle, inverse[...], upper[...])
        diagonal = jnp.sum(jnp.where(middle, upper[...], 0.0), axis=0, keepdims=True)
        out_ref[2 * h :, :] = jnp.broadcast_to(diagonal, (8, h))

    @pl.when(side_ref[0] == 0)
    def _():
        out_ref[:h, :] = mine_ref[:h, :]
        out_ref[h:, :] = jnp.zeros((h + 8, h), F32)


def first_factor(side, mine):
    h = mine.shape[1]
    return pl.pallas_call(
        first_kernel,
        out_shape=jax.ShapeDtypeStruct((2 * h + 8, h), F32),
        in_specs=[SMEM, VMEM],
        out_specs=VMEM,
        scratch_shapes=[pltpu.VMEM((h, h), F32)] * 3,
        compiler_params=params(),
        cost_estimate=pl.CostEstimate(flops=10 * h * h * h, bytes_accessed=8 * h * h, transcendentals=h),
    )(side, mine)


def basis_kernel(
    scale, side_ref, own_ref, sent_ref, rotation_ref, *refs
):
    sketched_refs, refs = refs[:PARTS], refs[PARTS:]
    basis_ref, triangle_ref, a, upper, inverse, rest, basis, triangle, sent = refs
    h = a.shape[0]
    rows = basis.shape[0]
    lower, middle = triangles((h, h))
    first = side_ref[0] == 0
    below = jnp.where(first, own_ref[:h, :], sent_ref[:h, :])
    corner = jnp.where(first, sent_ref[:h, :], own_ref[:h, :])
    factors = jnp.where(first, sent_ref[h:, :], own_ref[h:, :])
    inverse1 = jnp.where(lower | middle, factors[:h, :], 0.0)
    upper1 = jnp.where(lower, 0.0, jnp.where(middle, factors[h : h + 1, :], factors[:h, :]))
    left = dot_parts(below, inverse1, (1, 1))
    a[...] = corner - dot_parts(left, left, (1, 1))
    ahead = dot_parts(left, inverse1, (1, 0))
    triangle[:h, :h] = upper1 * (1.0 / scale)
    triangle[:h, h:] = left.T * (1.0 / scale)
    triangle[h:, :h] = jnp.zeros((h, h), F32)
    copies = [pltpu.make_async_copy(triangle.at[pl.ds(h * i, h)], triangle_ref.at[pl.ds(h * i, h)], sent.at[i]) for i in range(2)]
    copies[0].start()
    mapping = dot_parts(inverse1, scale * rotation_ref[:h, :], (0, 0))
    for i, ref in enumerate(sketched_refs):
        x1, x2, part = ref[:, :h], ref[:, h:], pl.ds(rows // PARTS * i, rows // PARTS)
        basis[part, :] = dot_parts(x1, mapping, (1, 0))
        rest[part, :] = stacked(x2 - dot_parts(x1, ahead, (1, 1)), LEFT, 1)
    turned = stacked(scale * rotation_ref[h:, :], RIGHT, 0)
    factor(a, upper, inverse)
    triangle[h:, h:] = upper[...] * (1.0 / scale)
    copies[1].start()
    mapping = stacked(product(stacked(inverse[...], LEFT, 0), turned, ((0,), (0,))), RIGHT, 0)
    step = rows // CHUNKS
    for i in range(CHUNKS):
        part = pl.ds(step * i, step)
        basis[part, :] += product(rest[part, :], mapping, ((1,), (0,)))
        copies.append(pltpu.make_async_copy(basis.at[part], basis_ref.at[part], sent.at[2 + i]))
        copies[-1].start()
    for copy in copies:
        copy.wait()


def basis_and_triangle(side, own, sent, rotation, sketched, scale):
    rows, n = sketched[0].shape[0] * PARTS, sketched[0].shape[1]
    h = n // 2
    return pl.pallas_call(
        functools.partial(basis_kernel, scale),
        out_shape=[jax.ShapeDtypeStruct((rows, n), F32), jax.ShapeDtypeStruct((n, n), F32)],
        in_specs=[SMEM] + [VMEM] * (3 + PARTS),
        out_specs=[pl.BlockSpec(memory_space=pltpu.HBM)] * 2,
        scratch_shapes=[pltpu.VMEM((h, h), F32)] * 3
        + [
            pltpu.VMEM((rows, len(LEFT) * h), BF16),
            pltpu.VMEM((rows, n), F32),
            pltpu.VMEM((n, n), F32),
            pltpu.SemaphoreType.DMA((2 + CHUNKS,)),
        ],
        compiler_params=params(),
        cost_estimate=pl.CostEstimate(
            flops=12 * rows * n * n + 40 * n * n * n, bytes_accessed=8 * rows * n + 12 * n * n, transcendentals=n
        ),
    )(side, own, sent, rotation, *sketched)


def shards(snapshots, sketch, rotation):
    depth = levels("tm")
    cells = snapshots.shape[0] * lax.axis_size("space")
    side = (lax.axis_index("tm").astype(jnp.int32) & 1).reshape(1)

    kept, near = {}, {}
    for mask in range(lax.axis_size("tm") - 2, 0, -2):
        *leaving, rows, held = sketch_leaving(mask | 1, mask, snapshots, sketch)
        near[mask] = [partner(part, 1) for part in leaving]
        kept[mask] = sketch_staying(rows, held)
    for level in range(1, depth):
        for mask in [m for m in kept if m >> level & 1]:
            leaving = [x + y for x, y in zip(kept.pop(mask), near.pop(mask))]
            arrived = [partner(part, 1 << level) for part in leaving]
            snapshots, *leaving = lax.optimization_barrier((snapshots, *leaving))
            if level < depth - 1:
                stays = mask ^ 1 << level
                near[stays] = [x + y for x, y in zip(near[stays], arrived)]
    *leaving, kept = sketch_last(snapshots, sketch)
    near = [partner(part, 1) for part in leaving]
    sketched, before = [], []
    for part in range(PARTS):
        count = SLICES // PARTS
        rows, *before = gram_part(part, side, kept, near[count * part : count * (part + 1)], arrived[part], *before)
        sketched.append(rows)
    mine, send = before
    mine = mine + partner(send, 1)
    flips = [1 << level for level in range(1, depth + levels("space"))]
    if len(flips) > 1:
        x, y, *flips = flips
        mine = mine + ((partner(mine, x | y) + partner(mine, x)) + partner(mine, y))
    for flip in flips:
        mine = mine + partner(mine, flip)
    own = first_factor(side, mine)
    return tuple(basis_and_triangle(side, own, partner(own, 1), rotation, sketched, math.sqrt(cells)))


def solution(mesh):
    in_specs = (P("space", "tm"), P("tm", None), P())
    out_specs = (P(("space", "tm"), None), P())
    return jax.shard_map(shards, mesh=mesh, in_specs=in_specs, out_specs=out_specs, check_vma=False)
```

```python
import functools
import math

import jax
import jax.numpy as jnp
from jax import lax
from jax.experimental import pallas as pl
from jax.experimental.pallas import tpu as pltpu
from jax.sharding import PartitionSpec as P

F32, BF16 = jnp.float32, jnp.bfloat16
VMEM = pl.BlockSpec(memory_space=pltpu.VMEM)
SMEM = pl.BlockSpec(memory_space=pltpu.SMEM)
BLOCK = 64
SLICES = 4
PARTS = 4
CHUNKS = 4
PANEL = 2


def params(mib=40):
    return pltpu.CompilerParams(vmem_limit_bytes=int(mib * 2**20))


AXES = ("space", "tm")


def partner(shard, flip):
    count = lax.axis_size("space") * lax.axis_size("tm")
    return lax.ppermute(shard, AXES, [(i, i ^ flip) for i in range(count)])


def levels(axis):
    return lax.axis_size(axis).bit_length() - 1


def split(x):
    high = x.astype(BF16)
    rest = x - high.astype(F32)
    middle = rest.astype(BF16)
    low = (rest - middle.astype(F32)).astype(BF16)
    return high, middle, low


def product(x, y, dims):
    return lax.dot_general(x, y, (dims, ((), ())), preferred_element_type=F32)


LEFT, RIGHT = (0, 0, 1, 0, 1, 2), (0, 1, 0, 2, 1, 0)


def stacked(x, order, axis):
    parts = split(x)
    return jnp.concatenate([parts[i] for i in order], axis=axis)


def dot_parts(x, y, over):
    return product(stacked(x, LEFT, over[0]), stacked(y, RIGHT, over[1]), ((over[0],), (over[1],)))


def triangles(shape):
    row = lax.broadcasted_iota(jnp.int32, shape, 0)
    column = lax.broadcasted_iota(jnp.int32, shape, 1)
    return row > column, row == column


def rows_of(ref, mask, rows):
    block = lax.axis_index("tm") ^ mask
    return ref.at[pl.ds(pl.multiple_of(block * rows, rows), rows)]


def in_hbm(x):
    return pltpu.with_memory_space_constraint(x, pltpu.HBM)


def leaving_kernel(leaves, stays, snapshots_ref, sketch_ref, *rest):
    *outs, next_ref, wide, tall, arrived = rest
    rows, step = tall.shape[0], outs[0].shape[0]
    copies = [
        pltpu.make_async_copy(sketch_ref, wide, arrived.at[0]),
        pltpu.make_async_copy(rows_of(snapshots_ref, leaves, rows), tall, arrived.at[1]),
        pltpu.make_async_copy(rows_of(snapshots_ref, stays, rows), next_ref, arrived.at[2]),
    ]
    for copy in copies:
        copy.start()
    copies[0].wait()
    copies[1].wait()
    for i, out in enumerate(outs):
        out[...] = jnp.dot(tall[step * i : step * (i + 1), :], wide[...], preferred_element_type=F32)
    copies[2].wait()


def sketch_leaving(leaves, stays, snapshots, sketch):
    rows = snapshots.shape[0] // lax.axis_size("tm")
    depth, columns = sketch.shape
    return pl.pallas_call(
        functools.partial(leaving_kernel, leaves, stays),
        out_shape=[jax.ShapeDtypeStruct((rows // PARTS, columns), F32)] * PARTS
        + [jax.ShapeDtypeStruct((rows, depth), BF16), jax.ShapeDtypeStruct((depth, columns), BF16)],
        in_specs=[pl.BlockSpec(memory_space=pltpu.HBM)] * 2,
        out_specs=[VMEM] * (PARTS + 2),
        scratch_shapes=[pltpu.VMEM((rows, depth), BF16), pltpu.SemaphoreType.DMA((3,))],
        compiler_params=params(),
        cost_estimate=pl.CostEstimate(
            flops=2 * rows * depth * columns, bytes_accessed=4 * rows * depth + 4 * depth * columns, transcendentals=0
        ),
    )(in_hbm(snapshots), in_hbm(sketch))


def staying_kernel(rows_ref, sketch_ref, *outs):
    step = outs[0].shape[0]
    for i, out in enumerate(outs):
        out[...] = jnp.dot(rows_ref[step * i : step * (i + 1), :], sketch_ref[...], preferred_element_type=F32)


def sketch_staying(rows, sketch):
    count, depth = rows.shape
    columns = sketch.shape[1]
    return pl.pallas_call(
        staying_kernel,
        out_shape=[jax.ShapeDtypeStruct((count // PARTS, columns), F32)] * PARTS,
        in_specs=[VMEM] * 2,
        out_specs=[VMEM] * PARTS,
        compiler_params=params(),
        cost_estimate=pl.CostEstimate(flops=2 * count * depth * columns, bytes_accessed=2 * count * depth, transcendentals=0),
    )(rows, sketch)


def last_kernel(snapshots_ref, sketch_ref, *refs):
    *outs, tall, wide, arrived = refs
    rows = tall.shape[0] // 2
    copies = [pltpu.make_async_copy(sketch_ref, wide, arrived.at[0])]
    for i in range(2):
        copies.append(pltpu.make_async_copy(rows_of(snapshots_ref, 1 - i, rows), tall.at[pl.ds(rows * i, rows)], arrived.at[1 + i]))
    for copy in copies:
        copy.start()
    copies[0].wait()
    place = 0
    for i, out in enumerate(outs):
        if i in (0, SLICES):
            copies[1 + i // SLICES].wait()
        count = out.shape[0]
        out[...] = jnp.dot(tall[place : place + count, :], wide[...], preferred_element_type=F32)
        place += count


def sketch_last(snapshots, sketch):
    rows = snapshots.shape[0] // lax.axis_size("tm")
    depth, columns = sketch.shape
    return pl.pallas_call(
        last_kernel,
        out_shape=[jax.ShapeDtypeStruct((rows // SLICES, columns), F32)] * SLICES + [jax.ShapeDtypeStruct((rows, columns), F32)],
        in_specs=[pl.BlockSpec(memory_space=pltpu.HBM)] * 2,
        out_specs=[VMEM] * (SLICES + 1),
        scratch_shapes=[
            pltpu.VMEM((2 * rows, depth), BF16),
            pltpu.VMEM((depth, columns), BF16),
            pltpu.SemaphoreType.DMA((3,)),
        ],
        compiler_params=params(),
        cost_estimate=pl.CostEstimate(flops=1, bytes_accessed=1, transcendentals=0),
    )(in_hbm(snapshots), in_hbm(sketch))


def gram_kernel(part, side_ref, kept_ref, far_ref, *rest):
    near_refs, rest = rest[: SLICES // PARTS], rest[SLICES // PARTS :]
    before, (sketched_ref, *outs) = rest[: min(part, 1)], rest[min(part, 1) :]
    count = far_ref.shape[0]
    mine = slice(count * part, count * (part + 1))
    sketched = (kept_ref[mine, :] + jnp.concatenate([ref[...] for ref in near_refs], axis=0)) + far_ref[...]
    sketched_ref[...] = sketched
    left, right = stacked(sketched, LEFT, 0), stacked(sketched, RIGHT, 0)
    h = sketched.shape[1] // 2
    rows = ((0,), (0,))
    top, bottom = product(left[:, :h], right[:, :h], rows), product(left[:, h:], right, rows)
    if before:
        top, bottom = top + before[0][:h, :h], bottom + before[0][h:, :]
    if part < PARTS - 1:
        (gram_ref,) = outs
        gram_ref[:h, :h] = top
        gram_ref[h:, :] = bottom
        return
    keep_ref, send_ref = outs
    lower, middle = triangles((h, h))
    corner = bottom[:, h:]
    diagonal = jnp.sum(jnp.where(middle, corner, 0.0), axis=0, keepdims=True)
    mixed = jnp.where(lower | middle, top, corner)
    first = side_ref[0] == 0
    keep_ref[:h, :] = jnp.where(first, bottom[:, :h], mixed)
    send_ref[:h, :] = jnp.where(first, mixed, bottom[:, :h])
    keep_ref[h:, :] = jnp.broadcast_to(diagonal, (8, h))
    send_ref[h:, :] = jnp.broadcast_to(diagonal, (8, h))


def gram_part(part, side, kept, near, far, *before):
    rows, n = far.shape
    half = jax.ShapeDtypeStruct((n // 2 + 8, n // 2), F32)
    outs = [half, half] if part == PARTS - 1 else [jax.ShapeDtypeStruct((n, n), F32)]
    return pl.pallas_call(
        functools.partial(gram_kernel, part),
        out_shape=[jax.ShapeDtypeStruct((rows, n), F32)] + outs,
        in_specs=[SMEM] + [VMEM] * (2 + len(near) + len(before)),
        out_specs=[VMEM] * (1 + len(outs)),
        compiler_params=params(),
        cost_estimate=pl.CostEstimate(
            flops=12 * rows * n * n, bytes_accessed=16 * rows * n + 4 * n * n, transcendentals=0
        ),
    )(side, kept, far, *near, *before)


def column(v, c):
    return jnp.broadcast_to(v[:, c : c + 1], (8, 128))


def row(v, k):
    return jnp.broadcast_to(v[k : k + 1, :], (8, 128))


def factor(a, upper, inverse):
    n = a.shape[0]
    tiles = n // 128
    lane = lax.broadcasted_iota(jnp.int32, (8, 128), 1)
    sub = lax.broadcasted_iota(jnp.int32, (8, 128), 0)
    groups, width = BLOCK // 8, 8 * PANEL
    zero = jnp.zeros((8, 128), F32)
    for start in range(0, n, BLOCK):
        tile, offset = divmod(start, 128)
        t = []
        for i in range(groups):
            top = start + 8 * i
            t.append([a[top : top + 8, 128 * x : 128 * x + 128] for x in range(tiles)])
            t[i].append(jnp.where(lane == sub + (offset + 8 * i), 1.0, 0.0))
        for q in range(0, groups, PANEL):
            first = offset + 8 * q
            c = {(g, j): column(t[q + g][tile], first + j) for g in range(PANEL) for j in range(8 * g + 8)}
            r, l, m = {}, {}, {}
            pivot = row(c[0, 0], 0)
            for j in range(width):
                r[j] = lax.rsqrt(pivot)
                if j + 1 < width:
                    g, k = divmod(j + 1, 8)
                    m[j + 1, j] = row(c[g, j], k) * r[j]
                    pivot = row(c[g, j + 1], k) - m[j + 1, j] * m[j + 1, j]
                for g in range(j // 8, PANEL):
                    l[g, j] = c[g, j] * r[j]
                for k in range(j + 1, width):
                    if k > j + 1:
                        m[k, j] = row(l[k // 8, j], k % 8)
                    for g in range(k // 8, PANEL):
                        c[g, k] = c[g, k] - l[g, j] * m[k, j]
            p = {}
            for g in range(PANEL):
                mine = t[q + g]
                for j in range(8 * g):
                    mine = [x - l[g, j] * y for x, y in zip(mine, p[j])]
                roots = r[8 * g]
                for jj in range(8):
                    j = 8 * g + jj
                    p[j] = [row(x, jj) * r[j] for x in mine]
                    below = jnp.where(sub > jj, l[g, j], 0.0)
                    mine = [x - below * y for x, y in zip(mine, p[j])]
                    roots = jnp.where(sub == jj, r[j], roots)
                t[q + g] = [x * roots for x in mine]
            for i in range(q + PANEL, groups):
                for g in range(PANEL):
                    c = [column(t[i][tile], first + 8 * g + jj) for jj in range(8)]
                    for jj in range(8):
                        c[jj] = c[jj] * r[8 * g + jj]
                        for kk in range(jj + 1, 8):
                            c[kk] = c[kk] - c[jj] * m[8 * g + kk, 8 * g + jj]
                    for jj in range(8):
                        t[i] = [x - c[jj] * y for x, y in zip(t[i], p[8 * g + jj])]
        done = (lane >= offset) & (lane < offset + BLOCK)
        left, right = [[] for _ in range(tiles)], [[] for _ in range(tiles)]
        for i in range(groups):
            top, own = start + 8 * i, t[i][tiles]
            for x in range(tiles):
                u = w = z = t[i][x]
                if x < tile:
                    u = zero
                elif x > tile:
                    w = zero
                else:
                    u = jnp.where(lane >= sub + (offset + 8 * i), u, 0.0)
                    w = jnp.where(lane < offset, w, own)
                    z = jnp.where(done, own, z)
                upper[top : top + 8, 128 * x : 128 * x + 128] = u
                inverse[top : top + 8, 128 * x : 128 * x + 128] = w
                left[x].append(u)
                right[x].append(z)
        after = start + BLOCK
        if after < n:
            y = jnp.concatenate([jnp.concatenate(v, axis=0) for v in right], axis=1)
            y = stacked(y, RIGHT, 0)
            for x in range(after // 128, tiles):
                update = product(stacked(jnp.concatenate(left[x], axis=0), LEFT, 0), y, ((0,), (0,)))
                for top in range(max(after, 128 * x), 128 * x + 128, 8):
                    for k in range(tiles):
                        old = a[top : top + 8, 128 * k : 128 * k + 128]
                        if k == tile:
                            old = jnp.where(done, 0.0, old)
                        new = update[top - 128 * x : top - 128 * x + 8, 128 * k : 128 * k + 128]
                        a[top : top + 8, 128 * k : 128 * k + 128] = old - new


def first_kernel(side_ref, mine_ref, out_ref, a, upper, inverse):
    h = a.shape[0]
    lower, middle = triangles((h, h))

    @pl.when(side_ref[0] == 1)
    def _():
        mixed = mine_ref[:h, :]
        flipped = mixed.T
        a[...] = jnp.where(lower | middle, mixed, flipped)
        out_ref[:h, :] = jnp.where(lower, flipped, jnp.where(middle, mine_ref[h : h + 1, :], mixed))
        factor(a, upper, inverse)
        out_ref[h : 2 * h, :] = jnp.where(lower | middle, inverse[...], upper[...])
        diagonal = jnp.sum(jnp.where(middle, upper[...], 0.0), axis=0, keepdims=True)
        out_ref[2 * h :, :] = jnp.broadcast_to(diagonal, (8, h))

    @pl.when(side_ref[0] == 0)
    def _():
        out_ref[:h, :] = mine_ref[:h, :]
        out_ref[h:, :] = jnp.zeros((h + 8, h), F32)


def first_factor(side, mine):
    h = mine.shape[1]
    return pl.pallas_call(
        first_kernel,
        out_shape=jax.ShapeDtypeStruct((2 * h + 8, h), F32),
        in_specs=[SMEM, VMEM],
        out_specs=VMEM,
        scratch_shapes=[pltpu.VMEM((h, h), F32)] * 3,
        compiler_params=params(),
        cost_estimate=pl.CostEstimate(flops=10 * h * h * h, bytes_accessed=8 * h * h, transcendentals=h),
    )(side, mine)


def basis_kernel(
    scale, side_ref, own_ref, sent_ref, rotation_ref, *refs
):
    sketched_refs, refs = refs[:PARTS], refs[PARTS:]
    basis_ref, triangle_ref, a, upper, inverse, rest, basis, triangle, sent = refs
    h = a.shape[0]
    rows = basis.shape[0]
    lower, middle = triangles((h, h))
    first = side_ref[0] == 0
    below = jnp.where(first, own_ref[:h, :], sent_ref[:h, :])
    corner = jnp.where(first, sent_ref[:h, :], own_ref[:h, :])
    factors = jnp.where(first, sent_ref[h:, :], own_ref[h:, :])
    inverse1 = jnp.where(lower | middle, factors[:h, :], 0.0)
    upper1 = jnp.where(lower, 0.0, jnp.where(middle, factors[h : h + 1, :], factors[:h, :]))
    left = dot_parts(below, inverse1, (1, 1))
    a[...] = corner - dot_parts(left, left, (1, 1))
    ahead = dot_parts(left, inverse1, (1, 0))
    triangle[:h, :h] = upper1 * (1.0 / scale)
    triangle[:h, h:] = left.T * (1.0 / scale)
    triangle[h:, :h] = jnp.zeros((h, h), F32)
    copies = [pltpu.make_async_copy(triangle.at[pl.ds(h * i, h)], triangle_ref.at[pl.ds(h * i, h)], sent.at[i]) for i in range(2)]
    copies[0].start()
    mapping = dot_parts(inverse1, scale * rotation_ref[:h, :], (0, 0))
    for i, ref in enumerate(sketched_refs):
        x1, x2, part = ref[:, :h], ref[:, h:], pl.ds(rows // PARTS * i, rows // PARTS)
        basis[part, :] = dot_parts(x1, mapping, (1, 0))
        rest[part, :] = stacked(x2 - dot_parts(x1, ahead, (1, 1)), LEFT, 1)
    turned = stacked(scale * rotation_ref[h:, :], RIGHT, 0)
    factor(a, upper, inverse)
    triangle[h:, h:] = upper[...] * (1.0 / scale)
    copies[1].start()
    mapping = stacked(product(stacked(inverse[...], LEFT, 0), turned, ((0,), (0,))), RIGHT, 0)
    step = rows // CHUNKS
    for i in range(CHUNKS):
        part = pl.ds(step * i, step)
        basis[part, :] += product(rest[part, :], mapping, ((1,), (0,)))
        copies.append(pltpu.make_async_copy(basis.at[part], basis_ref.at[part], sent.at[2 + i]))
        copies[-1].start()
    for copy in copies:
        copy.wait()


def basis_and_triangle(side, own, sent, rotation, sketched, scale):
    rows, n = sketched[0].shape[0] * PARTS, sketched[0].shape[1]
    h = n // 2
    return pl.pallas_call(
        functools.partial(basis_kernel, scale),
        out_shape=[jax.ShapeDtypeStruct((rows, n), F32), jax.ShapeDtypeStruct((n, n), F32)],
        in_specs=[SMEM] + [VMEM] * (3 + PARTS),
        out_specs=[pl.BlockSpec(memory_space=pltpu.HBM)] * 2,
        scratch_shapes=[pltpu.VMEM((h, h), F32)] * 3
        + [
            pltpu.VMEM((rows, len(LEFT) * h), BF16),
            pltpu.VMEM((rows, n), F32),
            pltpu.VMEM((n, n), F32),
            pltpu.SemaphoreType.DMA((2 + CHUNKS,)),
        ],
        compiler_params=params(),
        cost_estimate=pl.CostEstimate(
            flops=12 * rows * n * n + 40 * n * n * n, bytes_accessed=8 * rows * n + 12 * n * n, transcendentals=n
        ),
    )(side, own, sent, rotation, *sketched)


def shards(snapshots, sketch, rotation):
    depth = levels("tm")
    cells = snapshots.shape[0] * lax.axis_size("space")
    side = (lax.axis_index("tm").astype(jnp.int32) & 1).reshape(1)

    kept, near = {}, {}
    for mask in range(lax.axis_size("tm") - 2, 0, -2):
        *leaving, rows, held = sketch_leaving(mask | 1, mask, snapshots, sketch)
        near[mask] = [partner(part, 1) for part in leaving]
        kept[mask] = sketch_staying(rows, held)
    for level in range(1, depth):
        for mask in [m for m in kept if m >> level & 1]:
            leaving = [x + y for x, y in zip(kept.pop(mask), near.pop(mask))]
            arrived = [partner(part, 1 << level) for part in leaving]
            snapshots, *leaving = lax.optimization_barrier((snapshots, *leaving))
            if level < depth - 1:
                stays = mask ^ 1 << level
                near[stays] = [x + y for x, y in zip(near[stays], arrived)]
    *leaving, kept = sketch_last(snapshots, sketch)
    near = [partner(part, 1) for part in leaving]
    sketched, before = [], []
    for part in range(PARTS):
        count = SLICES // PARTS
        rows, *before = gram_part(part, side, kept, near[count * part : count * (part + 1)], arrived[part], *before)
        sketched.append(rows)
    mine, send = before
    mine = mine + partner(send, 1)
    flips = [1 << level for level in range(1, depth + levels("space"))]
    if len(flips) > 1:
        x, y, *flips = flips
        mine = mine + ((partner(mine, x | y) + partner(mine, y)) + partner(mine, x))
    for flip in flips:
        mine = mine + partner(mine, flip)
    own = first_factor(side, mine)
    return tuple(basis_and_triangle(side, own, partner(own, 1), rotation, sketched, math.sqrt(cells)))


def solution(mesh):
    in_specs = (P("space", "tm"), P("tm", None), P())
    out_specs = (P(("space", "tm"), None), P())
    return jax.shard_map(shards, mesh=mesh, in_specs=in_specs, out_specs=out_specs, check_vma=False)
```
